32 devices in a mesh: samp: 16 (over z, y, core), par: 2 (over x).
Axes of the slice: x: 2, y: 2, z: 4, core: 2. Of those that a mesh axis runs over, the one named last changes fastest.
Arguments:
- jacobian: float32 [4096, 8192], P('samp', 'par'), may hold values from -60 to 60, as said below
Outputs:
- gram: float32 [4096, 4096], P('samp', 'par')
The draws below stay inside these ranges and needn't reach their ends.
Inputs may be any that keep to these rules, and one draw needn't show every extreme that they name: `jacobian`: real-valued log-derivatives.
All inputs are finite; a program needn't handle non-finite values.
Results may differ from the reference program's by a relative error of at most 0.000065.
Values sent between devices are 32-bit elements; how exact they have to be, the bound alone decides.
A program may use at most 128 MiB of HBM per device.

```python
import jax
import jax.numpy as jnp
from jax import lax

P_SIZE = 8192
SAMPLES = 4096


def draw_jacobian(key, part):
    key = jax.random.fold_in(key, 7)
    k_rough, k_col, k_row, k_off = jax.random.split(key, 4)
    col_scale = jnp.exp(jax.random.uniform(k_col, (P_SIZE,), jnp.float32, jnp.log(0.3), jnp.log(3.0)))
    offset = jax.random.normal(k_off, (P_SIZE,), jnp.float32)
    ramp = 0.5 + jnp.arange(SAMPLES, dtype=jnp.float32) / SAMPLES
    rough = jax.random.normal(k_rough, (SAMPLES, P_SIZE), jnp.float32)
    row_scale = jnp.exp(jax.random.uniform(k_row, (SAMPLES,), jnp.float32, jnp.log(0.5), jnp.log(2.0)))
    rough = jnp.clip(rough, -6.0, 6.0)
    return row_scale[:, None] * col_scale[None, :] * rough + offset[None, :] * ramp[:, None]


def setup_inputs(seed: int = 0) -> dict:
    arg_keys = jax.random.split(jax.random.key(seed), 2)
    return {
        "jacobian": draw_jacobian(jax.random.fold_in(arg_keys[1], 71), 0),
    }


def reference(jacobian):
    mean = jnp.sum(jacobian, axis=0) / SAMPLES
    centred = jacobian - mean[None, :]
    product = jnp.dot(centred, centred.T, preferred_element_type=jnp.float32, precision=lax.Precision.HIGHEST)
    return product / SAMPLES
```

```python
import functools

import jax
import jax.numpy as jnp
from jax import lax
from jax.experimental import pallas as pl
from jax.experimental.pallas import tpu as pltpu
from jax.sharding import PartitionSpec as P

MESH = pl.DeviceIdType.MESH
GROUP = 4


def split(value):
    high = value.astype(jnp.bfloat16)
    low = (value - high.astype(jnp.float32)).astype(jnp.bfloat16)
    return high, low


def product(a_high, a_low, b_high, b_low):
    dims = (((1,), (1,)), ((), ()))
    dot = functools.partial(lax.dot_general, dimension_numbers=dims, preferred_element_type=jnp.float32)
    return dot(a_high, b_high) + (dot(a_high, b_low) + dot(a_low, b_high))


def kernel(
    planes, rows, width, samples,
    jac, out,
    own, high, low, other, sums, mean, part, core_in, y_in, x_in, near_in, far_in,
    copy_sem, swap_send, swap_recv, sum_send, sum_recv, line_send, line_recv,
    core_send, core_recv, y_send, y_recv, x_send, x_recv,
    near_send, near_recv, far_send, far_recv,
):
    half = width // 2
    per = planes // 2
    samp = lax.axis_index("samp")
    x = lax.axis_index("par")
    z = samp // GROUP
    q = samp % GROUP
    devices = planes * GROUP * 2
    me = samp * 2 + x

    def flip(a, k):
        low_a, high_a = a % 2, a // 2
        low_k, high_k = k % 2, k // 2
        return (low_a + low_k) % 2 + 2 * ((high_a + high_k) % 2)

    def remote(src, dst, send, recv, to_samp, to_par):
        return pltpu.make_async_remote_copy(
            src_ref=src, dst_ref=dst, send_sem=send, recv_sem=recv,
            device_id=(to_samp, to_par), device_id_type=MESH,
        )

    barrier = pltpu.get_barrier_semaphore()

    def greet(i, carry):
        @pl.when(i != me)
        def _():
            pl.semaphore_signal(barrier, inc=1, device_id=(i // 2, i % 2), device_id_type=MESH)
        return carry

    lax.fori_loop(0, devices, greet, 0)
    pl.semaphore_wait(barrier, devices - 1)

    def columns(i):
        return pl.ds(pl.multiple_of(i * width, width), width)

    def swap(k):
        to = flip(q, k)
        return remote(
            jac.at[:, columns(to)], own.at[q], swap_send.at[k], swap_recv.at[q], z * GROUP + to, x
        )

    def swap_in(k):
        return remote(
            jac.at[:, columns(q)], own.at[flip(q, k)], swap_send.at[k], swap_recv.at[flip(q, k)],
            z * GROUP + flip(q, k), x,
        )

    for k in (1, 2, 3):
        swap(k).start()
    mine = pltpu.make_async_copy(jac.at[:, columns(q)], own.at[q], copy_sem)
    mine.start()

    def left(plane, r, src):
        return remote(
            src, other.at[plane, r], line_send.at[0, plane, r], line_recv.at[plane, r],
            (z - 1) * GROUP + q, x,
        )

    def right(plane, r, src):
        return remote(
            src, other.at[plane, r], line_send.at[1, plane, r], line_recv.at[plane, r],
            (z + 1) * GROUP + q, x,
        )

    total = jnp.zeros((8, width), jnp.float32)
    for k in range(GROUP):
        r = flip(q, k)
        if k == 0:
            mine.wait()
        else:
            swap_in(k).wait_recv()

        @pl.when(z > 0)
        def _():
            left(z, r, own.at[r, :, pl.ds(0, half)]).start()

        @pl.when(z < planes - 1)
        def _():
            right(z, r, own.at[r, :, pl.ds(half, half)]).start()

        def add(i, acc):
            return acc + own[r, pl.ds(pl.multiple_of(i * 8, 8), 8), :]

        total = lax.fori_loop(0, rows // 8, add, total)
    sums[z] = total

    def sum_copy(plane, d):
        to = lax.rem(z + d, planes)
        return remote(
            sums.at[plane], sums.at[plane], sum_send.at[d], sum_recv.at[plane], to * GROUP + q, x
        )

    for d in range(1, planes):
        sum_copy(z, d).start()
    for d in range(1, planes):
        sum_copy(lax.rem(z + d, planes), d).wait_recv()
    whole = sums[0]
    for d in range(1, planes):
        whole = whole + sums[d]
    mean[...] = jnp.sum(whole, axis=0, keepdims=True) / samples

    @pl.loop(0, GROUP)
    def _(i):
        a, b = split(own[i] - mean[...])
        high[i] = a
        low[i] = b

    @pl.loop(0, GROUP * GROUP)
    def _(t):
        i, r = t // GROUP, t % GROUP
        part[z, i, r] = product(high[i], low[i], high[r], low[r])

    def multiply(plane, r, first):
        b_high, b_low = split(other[plane, r] - mean[:, pl.ds(first, half)])

        @pl.loop(0, GROUP)
        def _(i):
            part[plane, i, r] = product(
                high[i, :, pl.ds(first, half)], low[i, :, pl.ds(first, half)], b_high, b_low
            )

    def core_copy(plane, j):
        block = flip(q, 1 + 2 * j)
        return remote(
            part.at[plane, block], core_in.at[plane, j], core_send.at[plane, j],
            core_recv.at[plane, j], z * GROUP + flip(q, 1), x,
        )

    def y_copy(plane):
        return remote(
            part.at[plane, flip(q, 2)], y_in.at[plane], y_send.at[plane], y_recv.at[plane],
            z * GROUP + flip(q, 2), x,
        )

    def x_copy(plane):
        return remote(
            part.at[plane, q, pl.ds(2 * (1 - x), 2)], x_in.at[plane], x_send.at[plane],
            x_recv.at[plane], samp, 1 - x,
        )

    def near_copy(plane):
        return remote(
            part.at[plane, q, pl.ds(2 * x, 2)], near_in.at[plane % per], near_send.at[plane],
            near_recv.at[plane % per], samp, 1 - x,
        )

    def far_copy(plane, j):
        return remote(
            part.at[plane, q, 2 * x + j], far_in.at[z % per, q], far_send.at[plane, j],
            far_recv.at[z % per, q], plane * GROUP + 2 * x + j, z // per,
        )

    def stage0(plane):
        for j in (1, 0):
            core_copy(plane, j).start()

    def stage1(plane):
        core_copy(plane, 1).wait_recv()
        block = flip(q, 2)

        @pl.loop(0, GROUP)
        def _(r):
            part[plane, block, r] = part[plane, block, r] + core_in[plane, 1, r]

        y_copy(plane).start()
        core_copy(plane, 0).wait_recv()

        @pl.loop(0, GROUP)
        def _(r):
            part[plane, q, r] = part[plane, q, r] + core_in[plane, 0, r]

    def stage2(plane):
        y_copy(plane).wait_recv()

        @pl.loop(0, GROUP)
        def _(r):
            part[plane, q, r] = part[plane, q, r] + y_in[plane, r]

        x_copy(plane).start()

    def stage3(plane):
        x_copy(plane).wait_recv()
        for j in range(2):
            part[plane, q, 2 * x + j] = part[plane, q, 2 * x + j] + x_in[plane, j]

        @pl.when(plane // per != x)
        def _():
            near_copy(plane).start()

        @pl.when(plane != z)
        def _():
            for j in range(2):
                far_copy(plane, j).start()

    stages = (stage1, stage2, stage3)
    stage0(z)

    def step(t, carry):
        d, k = t // GROUP + 1, t % GROUP
        r = flip(q, k)
        before, after = z - d, z + d

        @pl.when(after < planes)
        def _():
            left(after, r, other.at[after, r]).wait_recv()

            @pl.when(z > 0)
            def _():
                left(after, r, other.at[after, r]).start()

        @pl.when(before >= 0)
        def _():
            right(before, r, other.at[before, r]).wait_recv()

            @pl.when(z < planes - 1)
            def _():
                right(before, r, other.at[before, r]).start()

        @pl.when(after < planes)
        def _():
            multiply(after, r, 0)

        @pl.when(before >= 0)
        def _():
            multiply(before, r, half)

        for i in range(3):
            @pl.when((k == i) & (d == 1))
            def _():
                stages[i](z)

            @pl.when((k == i) & (d > 1) & (after - 1 < planes))
            def _():
                stages[i](after - 1)

            @pl.when((k == i) & (d > 1) & (before + 1 >= 0))
            def _():
                stages[i](before + 1)

        @pl.when((k == GROUP - 1) & (after < planes))
        def _():
            stage0(after)

        @pl.when((k == GROUP - 1) & (before >= 0))
        def _():
            stage0(before)

        return carry

    lax.fori_loop(0, (planes - 1) * GROUP, step, 0)

    for last, exists in ((planes - 1, z == 0), (0, z == planes - 1)):
        @pl.when(exists)
        def _():
            for stage in stages:
                stage(last)

    for s in range(per):
        plane = x * per + s
        near_copy(plane).wait_recv()
        for r in range(GROUP):
            kept = part[plane, q, r]
            sent = near_in[s, r % 2]
            where = pl.ds((s * GROUP + r) * rows, rows)
            out[:, where] = jnp.where(x == r // 2, kept, sent) / samples

        @pl.when(plane != z)
        def _():
            for r in range(GROUP):
                remote(
                    part.at[plane, q, r], far_in.at[s, r], far_send.at[plane, 0], far_recv.at[s, r],
                    samp, 1 - x,
                ).wait_recv()
                where = pl.ds((s * GROUP + r) * rows, rows)
                out[:, where] = out[:, where] + far_in[s, r].T / samples

    for k in (1, 2, 3):
        swap(k).wait_send()
    for d in range(1, planes):
        sum_copy(z, d).wait_send()

    def drain(plane, carry):
        for r in range(GROUP):
            @pl.when((z > 0) & (plane >= z))
            def _():
                left(plane, r, other.at[plane, r]).wait_send()

            @pl.when((z < planes - 1) & (plane <= z))
            def _():
                right(plane, r, other.at[plane, r]).wait_send()

        for j in range(2):
            core_copy(plane, j).wait_send()
        y_copy(plane).wait_send()
        x_copy(plane).wait_send()

        @pl.when(plane // per != x)
        def _():
            near_copy(plane).wait_send()

        @pl.when(plane != z)
        def _():
            for j in range(2):
                far_copy(plane, j).wait_send()

        return carry

    lax.fori_loop(0, planes, drain, 0)


def lines(jacobian):
    rows, total = jacobian.shape
    count = lax.axis_size("samp")
    planes = count // GROUP
    per = planes // 2
    width = total // GROUP
    half = width // 2
    f32 = jnp.float32
    dma = pltpu.SemaphoreType.DMA
    body = functools.partial(kernel, planes, rows, width, float(rows * count))
    return pl.pallas_call(
        body,
        out_shape=jax.ShapeDtypeStruct((rows, per * GROUP * rows), f32),
        in_specs=[pl.BlockSpec(memory_space=pl.ANY)],
        out_specs=pl.BlockSpec(memory_space=pltpu.VMEM),
        scratch_shapes=[
            pltpu.VMEM((GROUP, rows, width), f32),
            pltpu.VMEM((GROUP, rows, width), jnp.bfloat16),
            pltpu.VMEM((GROUP, rows, width), jnp.bfloat16),
            pltpu.VMEM((planes, GROUP, rows, half), f32),
            pltpu.VMEM((planes, 8, width), f32),
            pltpu.VMEM((1, width), f32),
            pltpu.VMEM((planes, GROUP, GROUP, rows, rows), f32),
            pltpu.VMEM((planes, 2, GROUP, rows, rows), f32),
            pltpu.VMEM((planes, GROUP, rows, rows), f32),
            pltpu.VMEM((planes, 2, rows, rows), f32),
            pltpu.VMEM((per, 2, rows, rows), f32),
            pltpu.VMEM((per, GROUP, rows, rows), f32),
            dma,
            dma((GROUP,)), dma((GROUP,)),
            dma((planes,)), dma((planes,)),
            dma((2, planes, GROUP)), dma((planes, GROUP)),
            dma((planes, 2)), dma((planes, 2)),
            dma((planes,)), dma((planes,)),
            dma((planes,)), dma((planes,)),
            dma((planes,)), dma((per,)),
            dma((planes, 2)), dma((per, GROUP)),
        ],
        compiler_params=pltpu.CompilerParams(
            collective_id=0, has_side_effects=True, vmem_limit_bytes=60 * 2**20
        ),
    )(jacobian)


def tile_product(a, b):
    return jnp.dot(a, b.T, preferred_element_type=jnp.float32, precision=lax.Precision.HIGHEST)


def gathered(jacobian):
    rows = jacobian.shape[0]
    samples = rows * lax.axis_size("samp")
    totals = lax.psum(jnp.sum(jacobian, axis=0), "samp")
    centred = jacobian - (totals / samples)[None, :]
    partial_rows = tile_product(centred, lax.all_gather(centred, "samp", axis=0, tiled=True))
    return lax.psum_scatter(partial_rows, "par", scatter_dimension=1, tiled=True) / samples


def scratch_bytes(rows, total, planes):
    square = rows * rows * 4
    return rows * total * 4 * 2 + planes * rows * total * 2 + planes * square * 30 + planes * square * 5


def solution(mesh):
    planes, rest = divmod(mesh.shape["samp"], GROUP)

    def per_device(jacobian):
        rows, total = jacobian.shape
        fits = scratch_bytes(rows, total, planes) <= 56 * 2**20
        if mesh.shape["par"] == 2 and rest == 0 and planes % 2 == 0 and fits and total % 1024 == 0:
            return lines(jacobian)
        return gathered(jacobian)

    return jax.shard_map(
        per_device, mesh=mesh, in_specs=(P("samp", "par"),), out_specs=P("samp", "par"), check_vma=False
    )
```

```python
import functools

import jax
import jax.numpy as jnp
from jax import lax
from jax.experimental import pallas as pl
from jax.experimental.pallas import tpu as pltpu
from jax.sharding import PartitionSpec as P

MESH = pl.DeviceIdType.MESH
GROUP = 4


def split(value):
    high = value.astype(jnp.bfloat16)
    low = (value - high.astype(jnp.float32)).astype(jnp.bfloat16)
    return high, low


def product(a_high, a_low, b_high, b_low):
    dims = (((1,), (1,)), ((), ()))
    dot = functools.partial(lax.dot_general, dimension_numbers=dims, preferred_element_type=jnp.float32)
    return dot(a_high, b_high) + (dot(a_high, b_low) + dot(a_low, b_high))


def kernel(
    planes, rows, width, samples,
    jac, out,
    own, high, low, other, sums, mean, part, core_in, y_in, x_in, near_in, far_in,
    copy_sem, swap_send, swap_recv, sum_send, sum_recv, line_send, line_recv,
    core_send, core_recv, y_send, y_recv, x_send, x_recv,
    near_send, near_recv, far_send, far_recv,
):
    half = width // 2
    per = planes // 2
    samp = lax.axis_index("samp")
    x = lax.axis_index("par")
    z = samp // GROUP
    q = samp % GROUP
    devices = planes * GROUP * 2
    me = samp * 2 + x

    def flip(a, k):
        low_a, high_a = a % 2, a // 2
        low_k, high_k = k % 2, k // 2
        return (low_a + low_k) % 2 + 2 * ((high_a + high_k) % 2)

    def remote(src, dst, send, recv, to_samp, to_par):
        return pltpu.make_async_remote_copy(
            src_ref=src, dst_ref=dst, send_sem=send, recv_sem=recv,
            device_id=(to_samp, to_par), device_id_type=MESH,
        )

    barrier = pltpu.get_barrier_semaphore()

    def greet(i, carry):
        @pl.when(i != me)
        def _():
            pl.semaphore_signal(barrier, inc=1, device_id=(i // 2, i % 2), device_id_type=MESH)
        return carry

    lax.fori_loop(0, devices, greet, 0)
    pl.semaphore_wait(barrier, devices - 1)

    def columns(i, h):
        return pl.ds(pl.multiple_of(i * width + h * half, half), half)

    def swap(k, h):
        to = flip(q, k)
        return remote(
            jac.at[:, columns(to, h)], own.at[h, q], swap_send.at[k, h], swap_recv.at[q, h],
            z * GROUP + to, x,
        )

    def swap_in(k, h):
        source = flip(q, k)
        return remote(
            jac.at[:, columns(q, h)], own.at[h, source], swap_send.at[k, h],
            swap_recv.at[source, h], z * GROUP + source, x,
        )

    mine = [
        pltpu.make_async_copy(jac.at[:, columns(q, h)], own.at[h, q], copy_sem.at[h]) for h in (0, 1)
    ]
    for k in range(GROUP):
        for h in (0, 1):
            if k == 0:
                mine[h].start()
            else:
                swap(k, h).start()

    def left(plane, r, src):
        return remote(
            src, other.at[plane, r], line_send.at[0, plane, r], line_recv.at[plane, r],
            (z - 1) * GROUP + q, x,
        )

    def right(plane, r, src):
        return remote(
            src, other.at[plane, r], line_send.at[1, plane, r], line_recv.at[plane, r],
            (z + 1) * GROUP + q, x,
        )

    totals = [jnp.zeros((8, half), jnp.float32) for _ in range(2)]
    for k in range(GROUP):
        r = flip(q, k)
        for h in (0, 1):
            if k == 0:
                mine[h].wait()
            else:
                swap_in(k, h).wait_recv()

            @pl.when((z > 0) if h == 0 else (z < planes - 1))
            def _():
                (left if h == 0 else right)(z, r, own.at[h, r]).start()

            def add(i, acc):
                return acc + own[h, r, pl.ds(pl.multiple_of(i * 8, 8), 8), :]

            totals[h] = lax.fori_loop(0, rows // 8, add, totals[h])
    for h in (0, 1):
        sums[z, h] = totals[h]

    def sum_copy(plane, d):
        to = lax.rem(z + d, planes)
        return remote(
            sums.at[plane], sums.at[plane], sum_send.at[d], sum_recv.at[plane], to * GROUP + q, x
        )

    for d in range(1, planes):
        sum_copy(z, d).start()

    def relay(d, r):
        before, after = z - d, z + d

        @pl.when(after < planes)
        def _():
            left(after, r, other.at[after, r]).wait_recv()

            @pl.when(z > 0)
            def _():
                left(after, r, other.at[after, r]).start()

        @pl.when(before >= 0)
        def _():
            right(before, r, other.at[before, r]).wait_recv()

            @pl.when(z < planes - 1)
            def _():
                right(before, r, other.at[before, r]).start()

    for r in range(GROUP):
        relay(1, r)

    for d in range(1, planes):
        sum_copy(lax.rem(z + d, planes), d).wait_recv()
    for h in (0, 1):
        whole = sums[0, h]
        for d in range(1, planes):
            whole = whole + sums[d, h]
        mean[h] = jnp.sum(whole, axis=0, keepdims=True) / samples

    @pl.loop(0, GROUP)
    def _(i):
        for h in (0, 1):
            a, b = split(own[h, i] - mean[h])
            high[h, i] = a
            low[h, i] = b

    def square(r):
        @pl.loop(0, GROUP)
        def _(i):
            part[z, i, r] = product(high[0, i], low[0, i], high[0, r], low[0, r]) + product(
                high[1, i], low[1, i], high[1, r], low[1, r]
            )

    def multiply(plane, r, h):
        b_high, b_low = split(other[plane, r] - mean[h])

        @pl.loop(0, GROUP)
        def _(i):
            part[plane, i, r] = product(high[h, i], low[h, i], b_high, b_low)

    def core_copy(plane, r, j):
        block = flip(q, 1 + 2 * j)
        return remote(
            part.at[plane, block, r], core_in.at[plane, r, j], core_send.at[plane, r, j],
            core_recv.at[plane, r, j], z * GROUP + flip(q, 1), x,
        )

    def y_copy(plane, r):
        return remote(
            part.at[plane, flip(q, 2), r], y_in.at[plane, r], y_send.at[plane, r],
            y_recv.at[plane, r], z * GROUP + flip(q, 2), x,
        )

    def x_copy(plane, r):
        return remote(
            part.at[plane, q, r], x_in.at[plane, r % 2], x_send.at[plane, r],
            x_recv.at[plane, r], samp, 1 - x,
        )

    def near_copy(plane, r):
        return remote(
            part.at[plane, q, r], near_in.at[plane % per, r % 2], near_send.at[plane, r],
            near_recv.at[plane % per, r % 2], samp, 1 - x,
        )

    def far_copy(plane, r):
        return remote(
            part.at[plane, q, r], far_in.at[z % per, q], far_send.at[plane, r],
            far_recv.at[z % per, q], plane * GROUP + r, z // per,
        )

    def stage0(plane, r):
        for j in (1, 0):
            core_copy(plane, r, j).start()

    def stage1(plane, r):
        core_copy(plane, r, 1).wait_recv()
        block = flip(q, 2)
        part[plane, block, r] = part[plane, block, r] + core_in[plane, r, 1]
        y_copy(plane, r).start()
        core_copy(plane, r, 0).wait_recv()
        part[plane, q, r] = part[plane, q, r] + core_in[plane, r, 0]

    def stage2(plane, r):
        y_copy(plane, r).wait_recv()
        part[plane, q, r] = part[plane, q, r] + y_in[plane, r]

        @pl.when(r // 2 != x)
        def _():
            x_copy(plane, r).start()

    def stage3(plane, r):
        @pl.when(r // 2 == x)
        def _():
            x_copy(plane, r).wait_recv()
            part[plane, q, r] = part[plane, q, r] + x_in[plane, r % 2]

            @pl.when(plane // per != x)
            def _():
                near_copy(plane, r).start()

            @pl.when(plane != z)
            def _():
                far_copy(plane, r).start()

    steps = planes * GROUP

    def each(e, run):
        d, r = e // GROUP, e % GROUP

        @pl.when((e >= 0) & (e < steps) & (z + d < planes))
        def _():
            run(z + d, r)

        @pl.when((e >= GROUP) & (e < steps) & (z - d >= 0))
        def _():
            run(z - d, r)

    def step(e, carry):
        d, r = e // GROUP, e % GROUP
        each(e - 3, stage3)
        each(e - 2, stage2)
        each(e - 1, stage1)

        @pl.when((d > 1) & (d < planes))
        def _():
            relay(d, r)

        @pl.when(d == 0)
        def _():
            square(r)

        @pl.when((d > 0) & (z + d < planes))
        def _():
            multiply(z + d, r, 0)

        @pl.when((d > 0) & (z - d >= 0))
        def _():
            multiply(z - d, r, 1)

        each(e, stage0)
        return carry

    lax.fori_loop(0, steps + 3, step, 0)

    for s in range(per):
        plane = x * per + s
        for j in range(2):
            near_copy(plane, j).wait_recv()
        for r in range(GROUP):
            kept = part[plane, q, r]
            sent = near_in[s, r % 2]
            where = pl.ds((s * GROUP + r) * rows, rows)
            out[:, where] = jnp.where(x == r // 2, kept, sent) / samples

        @pl.when(plane != z)
        def _():
            for r in range(GROUP):
                remote(
                    part.at[plane, q, r], far_in.at[s, r], far_send.at[plane, r], far_recv.at[s, r],
                    samp, 1 - x,
                ).wait_recv()
                where = pl.ds((s * GROUP + r) * rows, rows)
                out[:, where] = out[:, where] + far_in[s, r].T / samples

    for k in (1, 2, 3):
        for h in (0, 1):
            swap(k, h).wait_send()
    for d in range(1, planes):
        sum_copy(z, d).wait_send()

    def drain(t, carry):
        plane, r = t // GROUP, t % GROUP

        @pl.when((z > 0) & (plane >= z))
        def _():
            left(plane, r, other.at[plane, r]).wait_send()

        @pl.when((z < planes - 1) & (plane <= z))
        def _():
            right(plane, r, other.at[plane, r]).wait_send()

        for j in range(2):
            core_copy(plane, r, j).wait_send()
        y_copy(plane, r).wait_send()

        @pl.when(r // 2 != x)
        def _():
            x_copy(plane, r).wait_send()

        @pl.when((r // 2 == x) & (plane // per != x))
        def _():
            near_copy(plane, r).wait_send()

        @pl.when((r // 2 == x) & (plane != z))
        def _():
            far_copy(plane, r).wait_send()

        return carry

    lax.fori_loop(0, steps, drain, 0)


def lines(jacobian):
    rows, total = jacobian.shape
    count = lax.axis_size("samp")
    planes = count // GROUP
    per = planes // 2
    width = total // GROUP
    half = width // 2
    f32 = jnp.float32
    dma = pltpu.SemaphoreType.DMA
    body = functools.partial(kernel, planes, rows, width, float(rows * count))
    return pl.pallas_call(
        body,
        out_shape=jax.ShapeDtypeStruct((rows, per * GROUP * rows), f32),
        in_specs=[pl.BlockSpec(memory_space=pl.ANY)],
        out_specs=pl.BlockSpec(memory_space=pltpu.VMEM),
        scratch_shapes=[
            pltpu.VMEM((2, GROUP, rows, half), f32),
            pltpu.VMEM((2, GROUP, rows, half), jnp.bfloat16),
            pltpu.VMEM((2, GROUP, rows, half), jnp.bfloat16),
            pltpu.VMEM((planes, GROUP, rows, half), f32),
            pltpu.VMEM((planes, 2, 8, half), f32),
            pltpu.VMEM((2, 1, half), f32),
            pltpu.VMEM((planes, GROUP, GROUP, rows, rows), f32),
            pltpu.VMEM((planes, GROUP, 2, rows, rows), f32),
            pltpu.VMEM((planes, GROUP, rows, rows), f32),
            pltpu.VMEM((planes, 2, rows, rows), f32),
            pltpu.VMEM((per, 2, rows, rows), f32),
            pltpu.VMEM((per, GROUP, rows, rows), f32),
            dma((2,)),
            dma((GROUP, 2)), dma((GROUP, 2)),
            dma((planes,)), dma((planes,)),
            dma((2, planes, GROUP)), dma((planes, GROUP)),
            dma((planes, GROUP, 2)), dma((planes, GROUP, 2)),
            dma((planes, GROUP)), dma((planes, GROUP)),
            dma((planes, GROUP)), dma((planes, GROUP)),
            dma((planes, GROUP)), dma((per, 2)),
            dma((planes, GROUP)), dma((per, GROUP)),
        ],
        compiler_params=pltpu.CompilerParams(
            collective_id=0, has_side_effects=True, vmem_limit_bytes=60 * 2**20
        ),
    )(jacobian)


def tile_product(a, b):
    return jnp.dot(a, b.T, preferred_element_type=jnp.float32, precision=lax.Precision.HIGHEST)


def gathered(jacobian):
    rows = jacobian.shape[0]
    samples = rows * lax.axis_size("samp")
    totals = lax.psum(jnp.sum(jacobian, axis=0), "samp")
    centred = jacobian - (totals / samples)[None, :]
    partial_rows = tile_product(centred, lax.all_gather(centred, "samp", axis=0, tiled=True))
    return lax.psum_scatter(partial_rows, "par", scatter_dimension=1, tiled=True) / samples


def scratch_bytes(rows, total, planes):
    square = rows * rows * 4
    return rows * total * 4 * 2 + planes * rows * total * 2 + planes * square * 30 + planes * square * 5


def solution(mesh):
    planes, rest = divmod(mesh.shape["samp"], GROUP)

    def per_device(jacobian):
        rows, total = jacobian.shape
        fits = scratch_bytes(rows, total, planes) <= 56 * 2**20
        if mesh.shape["par"] == 2 and rest == 0 and planes % 2 == 0 and fits and total % 1024 == 0:
            return lines(jacobian)
        return gathered(jacobian)

    return jax.shard_map(
        per_device, mesh=mesh, in_specs=(P("samp", "par"),), out_specs=P("samp", "par"), check_vma=False
    )
```

```python
import functools

import jax
import jax.numpy as jnp
from jax import lax
from jax.experimental import pallas as pl
from jax.experimental.pallas import tpu as pltpu
from jax.sharding import PartitionSpec as P

MESH = pl.DeviceIdType.MESH
GROUP = 4


def split(value):
    high = value.astype(jnp.bfloat16)
    low = (value - high.astype(jnp.float32)).astype(jnp.bfloat16)
    return high, low


def product(a_high, a_low, b_high, b_low):
    dims = (((1,), (1,)), ((), ()))
    dot = functools.partial(lax.dot_general, dimension_numbers=dims, preferred_element_type=jnp.float32)
    return dot(a_high, b_high) + (dot(a_high, b_low) + dot(a_low, b_high))


def kernel(
    planes, rows, width, samples,
    jac, out,
    own, high, low, other, sums, mean, part, core_in, y_in, x_in, near_in, far_in,
    copy_sem, swap_send, swap_recv, sum_send, sum_recv, line_send, line_recv,
    core_send, core_recv, y_send, y_recv, x_send, x_recv,
    near_send, near_recv, far_send, far_recv,
):
    half = width // 2
    per = planes // 2
    samp = lax.axis_index("samp")
    x = lax.axis_index("par")
    z = samp // GROUP
    q = samp % GROUP
    devices = planes * GROUP * 2
    me = samp * 2 + x

    def flip(a, k):
        low_a, high_a = a % 2, a // 2
        low_k, high_k = k % 2, k // 2
        return (low_a + low_k) % 2 + 2 * ((high_a + high_k) % 2)

    def remote(src, dst, send, recv, to_samp, to_par):
        return pltpu.make_async_remote_copy(
            src_ref=src, dst_ref=dst, send_sem=send, recv_sem=recv,
            device_id=(to_samp, to_par), device_id_type=MESH,
        )

    barrier = pltpu.get_barrier_semaphore()

    def greet(i, carry):
        @pl.when(i != me)
        def _():
            pl.semaphore_signal(barrier, inc=1, device_id=(i // 2, i % 2), device_id_type=MESH)
        return carry

    lax.fori_loop(0, devices, greet, 0)
    pl.semaphore_wait(barrier, devices - 1)

    def columns(i, h):
        return pl.ds(pl.multiple_of(i * width + h * half, half), half)

    def swap(k, h):
        to = flip(q, k)
        return remote(
            jac.at[:, columns(to, h)], own.at[h, q], swap_send.at[k, h], swap_recv.at[q, h],
            z * GROUP + to, x,
        )

    def swap_in(k, h):
        source = flip(q, k)
        return remote(
            jac.at[:, columns(q, h)], own.at[h, source], swap_send.at[k, h],
            swap_recv.at[source, h], z * GROUP + source, x,
        )

    mine = [
        pltpu.make_async_copy(jac.at[:, columns(q, h)], own.at[h, q], copy_sem.at[h]) for h in (0, 1)
    ]
    for k in range(GROUP):
        for h in (0, 1):
            if k == 0:
                mine[h].start()
            else:
                swap(k, h).start()

    def left(plane, r, src):
        return remote(
            src, other.at[plane, r], line_send.at[0, plane, r], line_recv.at[plane, r],
            (z - 1) * GROUP + q, x,
        )

    def right(plane, r, src):
        return remote(
            src, other.at[plane, r], line_send.at[1, plane, r], line_recv.at[plane, r],
            (z + 1) * GROUP + q, x,
        )

    totals = [jnp.zeros((8, half), jnp.float32) for _ in range(2)]
    for k in range(GROUP):
        r = flip(q, k)
        for h in (0, 1):
            if k == 0:
                mine[h].wait()
            else:
                swap_in(k, h).wait_recv()

            @pl.when((z > 0) if h == 0 else (z < planes - 1))
            def _():
                (left if h == 0 else right)(z, r, own.at[h, r]).start()

            def add(i, acc):
                return acc + own[h, r, pl.ds(pl.multiple_of(i * 8, 8), 8), :]

            totals[h] = lax.fori_loop(0, rows // 8, add, totals[h])
    for h in (0, 1):
        sums[z, h] = totals[h]

    def sum_copy(plane, d):
        to = lax.rem(z + d, planes)
        return remote(
            sums.at[plane], sums.at[plane], sum_send.at[d], sum_recv.at[plane], to * GROUP + q, x
        )

    for d in range(1, planes):
        sum_copy(z, d).start()

    def relay(d, r):
        before, after = z - d, z + d

        @pl.when(after < planes)
        def _():
            left(after, r, other.at[after, r]).wait_recv()

            @pl.when(z > 0)
            def _():
                left(after, r, other.at[after, r]).start()

        @pl.when(before >= 0)
        def _():
            right(before, r, other.at[before, r]).wait_recv()

            @pl.when(z < planes - 1)
            def _():
                right(before, r, other.at[before, r]).start()

    for r in range(GROUP):
        relay(1, r)

    for d in range(1, planes):
        sum_copy(lax.rem(z + d, planes), d).wait_recv()
    for h in (0, 1):
        whole = sums[0, h]
        for d in range(1, planes):
            whole = whole + sums[d, h]
        mean[h] = jnp.sum(whole, axis=0, keepdims=True) / samples

    @pl.loop(0, GROUP)
    def _(i):
        for h in (0, 1):
            a, b = split(own[h, i] - mean[h])
            high[h, i] = a
            low[h, i] = b

    def square(r):
        @pl.loop(0, GROUP)
        def _(i):
            part[z, i, r] = product(high[0, i], low[0, i], high[0, r], low[0, r]) + product(
                high[1, i], low[1, i], high[1, r], low[1, r]
            )

    def multiply(plane, r, h):
        b_high, b_low = split(other[plane, r] - mean[h])

        @pl.loop(0, GROUP)
        def _(i):
            part[plane, i, r] = product(high[h, i], low[h, i], b_high, b_low)

    def core_copy(plane, r, j):
        block = flip(q, 1 + 2 * j)
        return remote(
            part.at[plane, block, r], core_in.at[plane, r, j], core_send.at[plane, r, j],
            core_recv.at[plane, r, j], z * GROUP + flip(q, 1), x,
        )

    def y_copy(plane, r):
        return remote(
            part.at[plane, flip(q, 2), r], y_in.at[plane, r], y_send.at[plane, r],
            y_recv.at[plane, r], z * GROUP + flip(q, 2), x,
        )

    def x_copy(plane, r, j):
        return remote(
            part.at[plane, flip(q, 2 * j), r], x_in.at[plane, r % 2 + j], x_send.at[plane, r, j],
            x_recv.at[plane, r, j], samp, 1 - x,
        )

    def near_copy(plane, r):
        return remote(
            part.at[plane, q, r], near_in.at[plane % per, r % 2], near_send.at[plane, r],
            near_recv.at[plane % per, r % 2], samp, 1 - x,
        )

    def far_copy(plane, r):
        return remote(
            part.at[plane, q, r], far_in.at[z % per, q], far_send.at[plane, r],
            far_recv.at[z % per, q], plane * GROUP + r, z // per,
        )

    def stage0(plane, r):
        for j in (1, 0):
            core_copy(plane, r, j).start()

    def add_y(plane, r):
        y_copy(plane, r).wait_recv()
        part[plane, q, r] = part[plane, q, r] + y_in[plane, r]

    def add_x(plane, r, j):
        x_copy(plane, r, j).wait_recv()
        block = flip(q, 2 * j)
        part[plane, block, r] = part[plane, block, r] + x_in[plane, r % 2 + j]

    def stage1(plane, r):
        core_copy(plane, r, 1).wait_recv()
        block = flip(q, 2)
        part[plane, block, r] = part[plane, block, r] + core_in[plane, r, 1]

        @pl.when(r % 2 == 0)
        def _():
            y_copy(plane, r).start()

        @pl.when((r % 2 == 1) & (r // 2 != x))
        def _():
            x_copy(plane, r, 1).start()

        core_copy(plane, r, 0).wait_recv()
        part[plane, q, r] = part[plane, q, r] + core_in[plane, r, 0]

        @pl.when((r % 2 == 1) & (r // 2 != x))
        def _():
            x_copy(plane, r, 0).start()

    def stage2(plane, r):
        @pl.when(r % 2 == 0)
        def _():
            add_y(plane, r)

            @pl.when(r // 2 != x)
            def _():
                x_copy(plane, r, 0).start()

        @pl.when((r % 2 == 1) & (r // 2 == x))
        def _():
            add_x(plane, r, 1)
            y_copy(plane, r).start()
            add_x(plane, r, 0)

    def stage3(plane, r):
        @pl.when(r // 2 == x)
        def _():
            @pl.when(r % 2 == 0)
            def _():
                add_x(plane, r, 0)

            @pl.when(r % 2 == 1)
            def _():
                add_y(plane, r)

            @pl.when(plane // per != x)
            def _():
                near_copy(plane, r).start()

            @pl.when(plane != z)
            def _():
                far_copy(plane, r).start()

    steps = planes * GROUP

    def each(e, run):
        d, r = e // GROUP, e % GROUP

        @pl.when((e >= 0) & (e < steps) & (z + d < planes))
        def _():
            run(z + d, r)

        @pl.when((e >= GROUP) & (e < steps) & (z - d >= 0))
        def _():
            run(z - d, r)

    def step(e, carry):
        d, r = e // GROUP, e % GROUP
        for block in range(GROUP):
            early = 2 * GROUP - 1 - block // 2
            ahead = (e + early) // GROUP

            @pl.when(((e + early) % GROUP == block) & (ahead > 1) & (ahead < planes))
            def _():
                relay(ahead, block)

        each(e - 3, stage3)
        each(e - 2, stage2)
        each(e - 1, stage1)

        @pl.when(d == 0)
        def _():
            square(r)

        @pl.when((d > 0) & (z + d < planes))
        def _():
            multiply(z + d, r, 0)

        @pl.when((d > 0) & (z - d >= 0))
        def _():
            multiply(z - d, r, 1)

        each(e, stage0)
        return carry

    lax.fori_loop(0, steps + 3, step, 0)

    for s in range(per):
        plane = x * per + s
        for j in range(2):
            near_copy(plane, j).wait_recv()
        for r in range(GROUP):
            kept = part[plane, q, r]
            sent = near_in[s, r % 2]
            where = pl.ds((s * GROUP + r) * rows, rows)
            out[:, where] = jnp.where(x == r // 2, kept, sent) / samples

        @pl.when(plane != z)
        def _():
            for r in range(GROUP):
                remote(
                    part.at[plane, q, r], far_in.at[s, r], far_send.at[plane, r], far_recv.at[s, r],
                    samp, 1 - x,
                ).wait_recv()
                where = pl.ds((s * GROUP + r) * rows, rows)
                out[:, where] = out[:, where] + far_in[s, r].T / samples

    for k in (1, 2, 3):
        for h in (0, 1):
            swap(k, h).wait_send()
    for d in range(1, planes):
        sum_copy(z, d).wait_send()

    def drain(t, carry):
        plane, r = t // GROUP, t % GROUP

        @pl.when((z > 0) & (plane >= z))
        def _():
            left(plane, r, other.at[plane, r]).wait_send()

        @pl.when((z < planes - 1) & (plane <= z))
        def _():
            right(plane, r, other.at[plane, r]).wait_send()

        for j in range(2):
            core_copy(plane, r, j).wait_send()

        @pl.when((r % 2 == 0) | (r // 2 == x))
        def _():
            y_copy(plane, r).wait_send()

        @pl.when(r // 2 != x)
        def _():
            x_copy(plane, r, 0).wait_send()

            @pl.when(r % 2 == 1)
            def _():
                x_copy(plane, r, 1).wait_send()

        @pl.when((r // 2 == x) & (plane // per != x))
        def _():
            near_copy(plane, r).wait_send()

        @pl.when((r // 2 == x) & (plane != z))
        def _():
            far_copy(plane, r).wait_send()

        return carry

    lax.fori_loop(0, steps, drain, 0)


def lines(jacobian):
    rows, total = jacobian.shape
    count = lax.axis_size("samp")
    planes = count // GROUP
    per = planes // 2
    width = total // GROUP
    half = width // 2
    f32 = jnp.float32
    dma = pltpu.SemaphoreType.DMA
    body = functools.partial(kernel, planes, rows, width, float(rows * count))
    return pl.pallas_call(
        body,
        out_shape=jax.ShapeDtypeStruct((rows, per * GROUP * rows), f32),
        in_specs=[pl.BlockSpec(memory_space=pl.ANY)],
        out_specs=pl.BlockSpec(memory_space=pltpu.VMEM),
        scratch_shapes=[
            pltpu.VMEM((2, GROUP, rows, half), f32),
            pltpu.VMEM((2, GROUP, rows, half), jnp.bfloat16),
            pltpu.VMEM((2, GROUP, rows, half), jnp.bfloat16),
            pltpu.VMEM((planes, GROUP, rows, half), f32),
            pltpu.VMEM((planes, 2, 8, half), f32),
            pltpu.VMEM((2, 1, half), f32),
            pltpu.VMEM((planes, GROUP, GROUP, rows, rows), f32),
            pltpu.VMEM((planes, GROUP, 2, rows, rows), f32),
            pltpu.VMEM((planes, GROUP, rows, rows), f32),
            pltpu.VMEM((planes, 3, rows, rows), f32),
            pltpu.VMEM((per, 2, rows, rows), f32),
            pltpu.VMEM((per, GROUP, rows, rows), f32),
            dma((2,)),
            dma((GROUP, 2)), dma((GROUP, 2)),
            dma((planes,)), dma((planes,)),
            dma((2, planes, GROUP)), dma((planes, GROUP)),
            dma((planes, GROUP, 2)), dma((planes, GROUP, 2)),
            dma((planes, GROUP)), dma((planes, GROUP)),
            dma((planes, GROUP, 2)), dma((planes, GROUP, 2)),
            dma((planes, GROUP)), dma((per, 2)),
            dma((planes, GROUP)), dma((per, GROUP)),
        ],
        compiler_params=pltpu.CompilerParams(
            collective_id=0, has_side_effects=True, vmem_limit_bytes=60 * 2**20
        ),
    )(jacobian)


def tile_product(a, b):
    return jnp.dot(a, b.T, preferred_element_type=jnp.float32, precision=lax.Precision.HIGHEST)


def gathered(jacobian):
    rows = jacobian.shape[0]
    samples = rows * lax.axis_size("samp")
    totals = lax.psum(jnp.sum(jacobian, axis=0), "samp")
    centred = jacobian - (totals / samples)[None, :]
    partial_rows = tile_product(centred, lax.all_gather(centred, "samp", axis=0, tiled=True))
    return lax.psum_scatter(partial_rows, "par", scatter_dimension=1, tiled=True) / samples


def scratch_bytes(rows, total, planes):
    square = rows * rows * 4
    return rows * total * 4 * 2 + planes * rows * total * 2 + planes * square * 30 + planes * square * 5


def solution(mesh):
    planes, rest = divmod(mesh.shape["samp"], GROUP)

    def per_device(jacobian):
        rows, total = jacobian.shape
        fits = scratch_bytes(rows, total, planes) <= 56 * 2**20
        if mesh.shape["par"] == 2 and rest == 0 and planes % 2 == 0 and fits and total % 1024 == 0:
            return lines(jacobian)
        return gathered(jacobian)

    return jax.shard_map(
        per_device, mesh=mesh, in_specs=(P("samp", "par"),), out_specs=P("samp", "par"), check_vma=False
    )
```

```python
import functools

import jax
import jax.numpy as jnp
from jax import lax
from jax.experimental import pallas as pl
from jax.experimental.pallas import tpu as pltpu
from jax.sharding import PartitionSpec as P

MESH = pl.DeviceIdType.MESH
GROUP = 4


def split(value):
    high = value.astype(jnp.bfloat16)
    low = (value - high.astype(jnp.float32)).astype(jnp.bfloat16)
    return high, low


def product(a_high, a_low, b_high, b_low):
    dims = (((1,), (1,)), ((), ()))
    dot = functools.partial(lax.dot_general, dimension_numbers=dims, preferred_element_type=jnp.float32)
    return dot(a_high, b_high) + (dot(a_high, b_low) + dot(a_low, b_high))


def kernel(
    planes, rows, width, samples,
    jac, out,
    own, high, low, other, sums, mean, part, core_in, y_in, x_in, near_in, far_in,
    copy_sem, swap_send, swap_recv, sum_send, sum_recv, line_send, line_recv,
    core_send, core_recv, y_send, y_recv, x_send, x_recv,
    near_send, near_recv, far_send, far_recv,
):
    half = width // 2
    per = planes // 2
    samp = lax.axis_index("samp")
    x = lax.axis_index("par")
    z = samp // GROUP
    q = samp % GROUP
    devices = planes * GROUP * 2
    me = samp * 2 + x

    def flip(a, k):
        low_a, high_a = a % 2, a // 2
        low_k, high_k = k % 2, k // 2
        return (low_a + low_k) % 2 + 2 * ((high_a + high_k) % 2)

    def remote(src, dst, send, recv, to_samp, to_par):
        return pltpu.make_async_remote_copy(
            src_ref=src, dst_ref=dst, send_sem=send, recv_sem=recv,
            device_id=(to_samp, to_par), device_id_type=MESH,
        )

    barrier = pltpu.get_barrier_semaphore()

    def greet(i, carry):
        @pl.when(i != me)
        def _():
            pl.semaphore_signal(barrier, inc=1, device_id=(i // 2, i % 2), device_id_type=MESH)
        return carry

    lax.fori_loop(0, devices, greet, 0)
    pl.semaphore_wait(barrier, devices - 1)

    def columns(i, h):
        return pl.ds(pl.multiple_of(i * width + h * half, half), half)

    def swap(k, h):
        to = flip(q, k)
        return remote(
            jac.at[:, columns(to, h)], own.at[h, q], swap_send.at[k, h], swap_recv.at[q, h],
            z * GROUP + to, x,
        )

    def swap_in(k, h):
        source = flip(q, k)
        return remote(
            jac.at[:, columns(q, h)], own.at[h, source], swap_send.at[k, h],
            swap_recv.at[source, h], z * GROUP + source, x,
        )

    mine = [
        pltpu.make_async_copy(jac.at[:, columns(q, h)], own.at[h, q], copy_sem.at[h]) for h in (0, 1)
    ]
    for k in range(GROUP):
        for h in (0, 1):
            if k == 0:
                mine[h].start()
            else:
                swap(k, h).start()

    def left(plane, r, src):
        return remote(
            src, other.at[plane, r], line_send.at[0, plane, r], line_recv.at[plane, r],
            (z - 1) * GROUP + q, x,
        )

    def right(plane, r, src):
        return remote(
            src, other.at[plane, r], line_send.at[1, plane, r], line_recv.at[plane, r],
            (z + 1) * GROUP + q, x,
        )

    totals = [jnp.zeros((8, half), jnp.float32) for _ in range(2)]
    for k in range(GROUP):
        r = flip(q, k)
        for h in (0, 1):
            if k == 0:
                mine[h].wait()
            else:
                swap_in(k, h).wait_recv()

            @pl.when((z > 0) if h == 0 else (z < planes - 1))
            def _():
                (left if h == 0 else right)(z, r, own.at[h, r]).start()

            def add(i, acc):
                return acc + own[h, r, pl.ds(pl.multiple_of(i * 8, 8), 8), :]

            totals[h] = lax.fori_loop(0, rows // 8, add, totals[h])
    for h in (0, 1):
        sums[z, h] = totals[h]

    def sum_copy(plane, d):
        to = lax.rem(z + d, planes)
        return remote(
            sums.at[plane], sums.at[plane], sum_send.at[d], sum_recv.at[plane], to * GROUP + q, x
        )

    for d in range(1, planes):
        sum_copy(z, d).start()

    def relay(d, r, passes):
        before, after = z - d, z + d

        @pl.when((after < planes) & ((z > 0) == passes))
        def _():
            left(after, r, other.at[after, r]).wait_recv()
            if passes:
                left(after, r, other.at[after, r]).start()

        @pl.when((before >= 0) & ((z < planes - 1) == passes))
        def _():
            right(before, r, other.at[before, r]).wait_recv()
            if passes:
                right(before, r, other.at[before, r]).start()

    for r in range(GROUP):
        relay(1, r, True)

    for d in range(1, planes):
        sum_copy(lax.rem(z + d, planes), d).wait_recv()
    for h in (0, 1):
        whole = sums[0, h]
        for d in range(1, planes):
            whole = whole + sums[d, h]
        mean[h] = jnp.sum(whole, axis=0, keepdims=True) / samples

    @pl.loop(0, GROUP)
    def _(i):
        for h in (0, 1):
            a, b = split(own[h, i] - mean[h])
            high[h, i] = a
            low[h, i] = b

    def square(r):
        @pl.loop(0, GROUP)
        def _(i):
            part[z, i, r] = product(high[0, i], low[0, i], high[0, r], low[0, r]) + product(
                high[1, i], low[1, i], high[1, r], low[1, r]
            )

    def multiply(plane, r, h):
        b_high, b_low = split(other[plane, r] - mean[h])

        @pl.loop(0, GROUP)
        def _(i):
            part[plane, i, r] = product(high[h, i], low[h, i], b_high, b_low)

    def core_copy(plane, r, j):
        block = flip(q, 1 + 2 * j)
        return remote(
            part.at[plane, block, r], core_in.at[plane, r, j], core_send.at[plane, r, j],
            core_recv.at[plane, r, j], z * GROUP + flip(q, 1), x,
        )

    def y_copy(plane, r):
        return remote(
            part.at[plane, flip(q, 2), r], y_in.at[plane, r], y_send.at[plane, r],
            y_recv.at[plane, r], z * GROUP + flip(q, 2), x,
        )

    def x_copy(plane, r, j):
        return remote(
            part.at[plane, flip(q, 2 * j), r], x_in.at[plane, r % 2 + j], x_send.at[plane, r, j],
            x_recv.at[plane, r, j], samp, 1 - x,
        )

    def near_copy(plane, r):
        return remote(
            part.at[plane, q, r], near_in.at[plane % per, r % 2], near_send.at[plane, r],
            near_recv.at[plane % per, r % 2], samp, 1 - x,
        )

    def far_copy(plane, r):
        return remote(
            part.at[plane, q, r], far_in.at[z % per, q], far_send.at[plane, r],
            far_recv.at[z % per, q], plane * GROUP + r, z // per,
        )

    def stage0(plane, r):
        for j in (1, 0):
            core_copy(plane, r, j).start()

    def add_y(plane, r):
        y_copy(plane, r).wait_recv()
        part[plane, q, r] = part[plane, q, r] + y_in[plane, r]

    def add_x(plane, r, j):
        x_copy(plane, r, j).wait_recv()
        block = flip(q, 2 * j)
        part[plane, block, r] = part[plane, block, r] + x_in[plane, r % 2 + j]

    def stage1(plane, r):
        core_copy(plane, r, 1).wait_recv()
        block = flip(q, 2)
        part[plane, block, r] = part[plane, block, r] + core_in[plane, r, 1]

        @pl.when(r % 2 == 0)
        def _():
            y_copy(plane, r).start()

        @pl.when((r % 2 == 1) & (r // 2 != x))
        def _():
            x_copy(plane, r, 1).start()

        core_copy(plane, r, 0).wait_recv()
        part[plane, q, r] = part[plane, q, r] + core_in[plane, r, 0]

        @pl.when((r % 2 == 1) & (r // 2 != x))
        def _():
            x_copy(plane, r, 0).start()

    def stage2(plane, r):
        @pl.when(r % 2 == 0)
        def _():
            add_y(plane, r)

            @pl.when(r // 2 != x)
            def _():
                x_copy(plane, r, 0).start()

        @pl.when((r % 2 == 1) & (r // 2 == x))
        def _():
            add_x(plane, r, 1)
            y_copy(plane, r).start()
            add_x(plane, r, 0)

    def stage3(plane, r):
        @pl.when(r // 2 == x)
        def _():
            @pl.when(r % 2 == 0)
            def _():
                add_x(plane, r, 0)

            @pl.when(r % 2 == 1)
            def _():
                add_y(plane, r)

            @pl.when(plane // per != x)
            def _():
                near_copy(plane, r).start()

            @pl.when(plane != z)
            def _():
                far_copy(plane, r).start()

    steps = planes * GROUP

    def each(e, run):
        d, r = e // GROUP, e % GROUP

        @pl.when((e >= 0) & (e < steps) & (z + d < planes))
        def _():
            run(z + d, r)

        @pl.when((e >= GROUP) & (e < steps) & (z - d >= 0))
        def _():
            run(z - d, r)

    def step(e, carry):
        d, r = e // GROUP, e % GROUP
        for block in range(GROUP):
            early = 2 * GROUP - 1 - block // 2
            ahead = (e + early) // GROUP

            @pl.when(((e + early) % GROUP == block) & (ahead > 1) & (ahead < planes))
            def _():
                relay(ahead, block, True)

        each(e - 3, stage3)
        each(e - 2, stage2)
        each(e - 1, stage1)

        @pl.when((d > 0) & (d < planes))
        def _():
            relay(d, r, False)

        @pl.when(d == 0)
        def _():
            square(r)

        @pl.when((d > 0) & (z + d < planes))
        def _():
            multiply(z + d, r, 0)

        @pl.when((d > 0) & (z - d >= 0))
        def _():
            multiply(z - d, r, 1)

        each(e, stage0)
        return carry

    lax.fori_loop(0, steps + 3, step, 0)

    for s in range(per):
        plane = x * per + s
        for j in range(2):
            near_copy(plane, j).wait_recv()
        for r in range(GROUP):
            kept = part[plane, q, r]
            sent = near_in[s, r % 2]
            where = pl.ds((s * GROUP + r) * rows, rows)
            out[:, where] = jnp.where(x == r // 2, kept, sent) / samples

        @pl.when(plane != z)
        def _():
            for r in range(GROUP):
                remote(
                    part.at[plane, q, r], far_in.at[s, r], far_send.at[plane, r], far_recv.at[s, r],
                    samp, 1 - x,
                ).wait_recv()
                where = pl.ds((s * GROUP + r) * rows, rows)
                out[:, where] = out[:, where] + far_in[s, r].T / samples

    for k in (1, 2, 3):
        for h in (0, 1):
            swap(k, h).wait_send()
    for d in range(1, planes):
        sum_copy(z, d).wait_send()

    def drain(t, carry):
        plane, r = t // GROUP, t % GROUP

        @pl.when((z > 0) & (plane >= z))
        def _():
            left(plane, r, other.at[plane, r]).wait_send()

        @pl.when((z < planes - 1) & (plane <= z))
        def _():
            right(plane, r, other.at[plane, r]).wait_send()

        for j in range(2):
            core_copy(plane, r, j).wait_send()

        @pl.when((r % 2 == 0) | (r // 2 == x))
        def _():
            y_copy(plane, r).wait_send()

        @pl.when(r // 2 != x)
        def _():
            x_copy(plane, r, 0).wait_send()

            @pl.when(r % 2 == 1)
            def _():
                x_copy(plane, r, 1).wait_send()

        @pl.when((r // 2 == x) & (plane // per != x))
        def _():
            near_copy(plane, r).wait_send()

        @pl.when((r // 2 == x) & (plane != z))
        def _():
            far_copy(plane, r).wait_send()

        return carry

    lax.fori_loop(0, steps, drain, 0)


def lines(jacobian):
    rows, total = jacobian.shape
    count = lax.axis_size("samp")
    planes = count // GROUP
    per = planes // 2
    width = total // GROUP
    half = width // 2
    f32 = jnp.float32
    dma = pltpu.SemaphoreType.DMA
    body = functools.partial(kernel, planes, rows, width, float(rows * count))
    return pl.pallas_call(
        body,
        out_shape=jax.ShapeDtypeStruct((rows, per * GROUP * rows), f32),
        in_specs=[pl.BlockSpec(memory_space=pl.ANY)],
        out_specs=pl.BlockSpec(memory_space=pltpu.VMEM),
        scratch_shapes=[
            pltpu.VMEM((2, GROUP, rows, half), f32),
            pltpu.VMEM((2, GROUP, rows, half), jnp.bfloat16),
            pltpu.VMEM((2, GROUP, rows, half), jnp.bfloat16),
            pltpu.VMEM((planes, GROUP, rows, half), f32),
            pltpu.VMEM((planes, 2, 8, half), f32),
            pltpu.VMEM((2, 1, half), f32),
            pltpu.VMEM((planes, GROUP, GROUP, rows, rows), f32),
            pltpu.VMEM((planes, GROUP, 2, rows, rows), f32),
            pltpu.VMEM((planes, GROUP, rows, rows), f32),
            pltpu.VMEM((planes, 3, rows, rows), f32),
            pltpu.VMEM((per, 2, rows, rows), f32),
            pltpu.VMEM((per, GROUP, rows, rows), f32),
            dma((2,)),
            dma((GROUP, 2)), dma((GROUP, 2)),
            dma((planes,)), dma((planes,)),
            dma((2, planes, GROUP)), dma((planes, GROUP)),
            dma((planes, GROUP, 2)), dma((planes, GROUP, 2)),
            dma((planes, GROUP)), dma((planes, GROUP)),
            dma((planes, GROUP, 2)), dma((planes, GROUP, 2)),
            dma((planes, GROUP)), dma((per, 2)),
            dma((planes, GROUP)), dma((per, GROUP)),
        ],
        compiler_params=pltpu.CompilerParams(
            collective_id=0, has_side_effects=True, vmem_limit_bytes=60 * 2**20
        ),
    )(jacobian)


def tile_product(a, b):
    return jnp.dot(a, b.T, preferred_element_type=jnp.float32, precision=lax.Precision.HIGHEST)


def gathered(jacobian):
    rows = jacobian.shape[0]
    samples = rows * lax.axis_size("samp")
    totals = lax.psum(jnp.sum(jacobian, axis=0), "samp")
    centred = jacobian - (totals / samples)[None, :]
    partial_rows = tile_product(centred, lax.all_gather(centred, "samp", axis=0, tiled=True))
    return lax.psum_scatter(partial_rows, "par", scatter_dimension=1, tiled=True) / samples


def scratch_bytes(rows, total, planes):
    square = rows * rows * 4
    return rows * total * 4 * 2 + planes * rows * total * 2 + planes * square * 30 + planes * square * 5


def solution(mesh):
    planes, rest = divmod(mesh.shape["samp"], GROUP)

    def per_device(jacobian):
        rows, total = jacobian.shape
        fits = scratch_bytes(rows, total, planes) <= 56 * 2**20
        if mesh.shape["par"] == 2 and rest == 0 and planes % 2 == 0 and fits and total % 1024 == 0:
            return lines(jacobian)
        return gathered(jacobian)

    return jax.shard_map(
        per_device, mesh=mesh, in_specs=(P("samp", "par"),), out_specs=P("samp", "par"), check_vma=False
    )
```

```python
import functools

import jax
import jax.numpy as jnp
from jax import lax
from jax.experimental import pallas as pl
from jax.experimental.pallas import tpu as pltpu
from jax.sharding import PartitionSpec as P

MESH = pl.DeviceIdType.MESH
GROUP = 4


def split(value):
    high = value.astype(jnp.bfloat16)
    low = (value - high.astype(jnp.float32)).astype(jnp.bfloat16)
    return high, low


def product(a_high, a_low, b_high, b_low):
    dims = (((1,), (1,)), ((), ()))
    dot = functools.partial(lax.dot_general, dimension_numbers=dims, preferred_element_type=jnp.float32)
    return dot(a_high, b_high) + (dot(a_high, b_low) + dot(a_low, b_high))


def kernel(
    planes, rows, width, samples,
    jac, out,
    own, high, low, other, sums, mean, part, core_in, y_in, x_in, near_in, far_in,
    copy_sem, swap_send, swap_recv, sum_send, sum_recv, line_send, line_recv,
    core_send, core_recv, y_send, y_recv, x_send, x_recv,
    near_send, near_recv, far_send, far_recv,
):
    half = width // 2
    per = planes // 2
    samp = lax.axis_index("samp")
    x = lax.axis_index("par")
    z = samp // GROUP
    q = samp % GROUP
    devices = planes * GROUP * 2
    me = samp * 2 + x

    def flip(a, k):
        low_a, high_a = a % 2, a // 2
        low_k, high_k = k % 2, k // 2
        return (low_a + low_k) % 2 + 2 * ((high_a + high_k) % 2)

    def remote(src, dst, send, recv, to_samp, to_par):
        return pltpu.make_async_remote_copy(
            src_ref=src, dst_ref=dst, send_sem=send, recv_sem=recv,
            device_id=(to_samp, to_par), device_id_type=MESH,
        )

    barrier = pltpu.get_barrier_semaphore()

    def greet(i, carry):
        @pl.when(i != me)
        def _():
            pl.semaphore_signal(barrier, inc=1, device_id=(i // 2, i % 2), device_id_type=MESH)
        return carry

    lax.fori_loop(0, devices, greet, 0)
    pl.semaphore_wait(barrier, devices - 1)

    def columns(i, h):
        return pl.ds(pl.multiple_of(i * width + h * half, half), half)

    def swap(k, h):
        to = flip(q, k)
        return remote(
            jac.at[:, columns(to, h)], own.at[h, q], swap_send.at[k, h], swap_recv.at[q, h],
            z * GROUP + to, x,
        )

    def swap_in(k, h):
        source = flip(q, k)
        return remote(
            jac.at[:, columns(q, h)], own.at[h, source], swap_send.at[k, h],
            swap_recv.at[source, h], z * GROUP + source, x,
        )

    mine = [
        pltpu.make_async_copy(jac.at[:, columns(q, h)], own.at[h, q], copy_sem.at[h]) for h in (0, 1)
    ]
    for k in range(GROUP):
        for h in (0, 1):
            if k == 0:
                mine[h].start()
            else:
                swap(k, h).start()

    def left(plane, r, src):
        return remote(
            src, other.at[plane, r], line_send.at[0, plane, r], line_recv.at[plane, r],
            (z - 1) * GROUP + q, x,
        )

    def right(plane, r, src):
        return remote(
            src, other.at[plane, r], line_send.at[1, plane, r], line_recv.at[plane, r],
            (z + 1) * GROUP + q, x,
        )

    totals = [jnp.zeros((8, half), jnp.float32) for _ in range(2)]
    for k in range(GROUP):
        r = flip(q, k)
        for h in (0, 1):
            if k == 0:
                mine[h].wait()
            else:
                swap_in(k, h).wait_recv()

            @pl.when((z > 0) if h == 0 else (z < planes - 1))
            def _():
                (left if h == 0 else right)(z, r, own.at[h, r]).start()

            def add(i, acc):
                return acc + own[h, r, pl.ds(pl.multiple_of(i * 8, 8), 8), :]

            totals[h] = lax.fori_loop(0, rows // 8, add, totals[h])
    for h in (0, 1):
        sums[z, h] = totals[h]

    def sum_copy(plane, d):
        to = lax.rem(z + d, planes)
        return remote(
            sums.at[plane], sums.at[plane], sum_send.at[d], sum_recv.at[plane], to * GROUP + q, x
        )

    for d in range(1, planes):
        sum_copy(z, d).start()

    def relay(d, r, passes):
        before, after = z - d, z + d

        @pl.when((after < planes) & ((z > 0) == passes))
        def _():
            left(after, r, other.at[after, r]).wait_recv()
            if passes:
                left(after, r, other.at[after, r]).start()

        @pl.when((before >= 0) & ((z < planes - 1) == passes))
        def _():
            right(before, r, other.at[before, r]).wait_recv()
            if passes:
                right(before, r, other.at[before, r]).start()

    for r in range(GROUP):
        relay(1, r, True)

    for d in range(1, planes):
        sum_copy(lax.rem(z + d, planes), d).wait_recv()
    for h in (0, 1):
        whole = sums[0, h]
        for d in range(1, planes):
            whole = whole + sums[d, h]
        mean[h] = jnp.sum(whole, axis=0, keepdims=True) / samples

    @pl.loop(0, GROUP)
    def _(i):
        for h in (0, 1):
            a, b = split(own[h, i] - mean[h])
            high[h, i] = a
            low[h, i] = b

    def square(r):
        @pl.loop(0, GROUP)
        def _(i):
            part[z, i, r] = product(high[0, i], low[0, i], high[0, r], low[0, r]) + product(
                high[1, i], low[1, i], high[1, r], low[1, r]
            )

    def multiply(plane, r, h):
        b_high, b_low = split(other[plane, r] - mean[h])

        @pl.loop(0, GROUP)
        def _(i):
            part[plane, i, r] = product(high[h, i], low[h, i], b_high, b_low)

    def core_copy(plane, r, j):
        block = flip(q, 1 + 2 * j)
        return remote(
            part.at[plane, block, r], core_in.at[plane, r, j], core_send.at[plane, r, j],
            core_recv.at[plane, r, j], z * GROUP + flip(q, 1), x,
        )

    def y_copy(plane, r):
        return remote(
            part.at[plane, flip(q, 2), r], y_in.at[plane, r], y_send.at[plane, r],
            y_recv.at[plane, r], z * GROUP + flip(q, 2), x,
        )

    def x_copy(plane, r):
        return remote(
            part.at[plane, q, r], x_in.at[plane, r % 2], x_send.at[plane, r],
            x_recv.at[plane, r], samp, 1 - x,
        )

    def near_copy(plane, r):
        return remote(
            part.at[plane, q, r], near_in.at[plane % per, r % 2], near_send.at[plane, r],
            near_recv.at[plane % per, r % 2], samp, 1 - x,
        )

    def far_copy(plane, r):
        return remote(
            part.at[plane, q, r], far_in.at[z % per, q], far_send.at[plane, r],
            far_recv.at[z % per, q], plane * GROUP + r, z // per,
        )

    def stage0(plane, r):
        for j in (1, 0):
            core_copy(plane, r, j).start()

    def stage1(plane, r):
        core_copy(plane, r, 1).wait_recv()
        block = flip(q, 2)
        part[plane, block, r] = part[plane, block, r] + core_in[plane, r, 1]
        y_copy(plane, r).start()
        core_copy(plane, r, 0).wait_recv()
        part[plane, q, r] = part[plane, q, r] + core_in[plane, r, 0]

    def stage2(plane, r):
        y_copy(plane, r).wait_recv()
        part[plane, q, r] = part[plane, q, r] + y_in[plane, r]

        @pl.when(r // 2 != x)
        def _():
            x_copy(plane, r).start()

    def stage3(plane, r):
        @pl.when(r // 2 == x)
        def _():
            x_copy(plane, r).wait_recv()
            part[plane, q, r] = part[plane, q, r] + x_in[plane, r % 2]

            @pl.when(plane // per != x)
            def _():
                near_copy(plane, r).start()

            @pl.when(plane != z)
            def _():
                far_copy(plane, r).start()

    steps = planes * GROUP

    def each(e, run):
        d, r = e // GROUP, e % GROUP

        @pl.when((e >= 0) & (e < steps) & (z + d < planes))
        def _():
            run(z + d, r)

        @pl.when((e >= GROUP) & (e < steps) & (z - d >= 0))
        def _():
            run(z - d, r)

    def step(e, carry):
        d, r = e // GROUP, e % GROUP
        @pl.when((d > 0) & (d + 1 < planes))
        def _():
            relay(d + 1, r, True)

        each(e - 3, stage3)
        each(e - 2, stage2)
        each(e - 1, stage1)

        @pl.when((d > 0) & (d < planes))
        def _():
            relay(d, r, False)

        @pl.when(d == 0)
        def _():
            square(r)

        @pl.when((d > 0) & (z + d < planes))
        def _():
            multiply(z + d, r, 0)

        @pl.when((d > 0) & (z - d >= 0))
        def _():
            multiply(z - d, r, 1)

        each(e, stage0)
        return carry

    lax.fori_loop(0, steps + 3, step, 0)

    for s in range(per):
        plane = x * per + s
        for j in range(2):
            near_copy(plane, j).wait_recv()
        for r in range(GROUP):
            kept = part[plane, q, r]
            sent = near_in[s, r % 2]
            where = pl.ds((s * GROUP + r) * rows, rows)
            out[:, where] = jnp.where(x == r // 2, kept, sent) / samples

        @pl.when(plane != z)
        def _():
            for r in range(GROUP):
                remote(
                    part.at[plane, q, r], far_in.at[s, r], far_send.at[plane, r], far_recv.at[s, r],
                    samp, 1 - x,
                ).wait_recv()
                where = pl.ds((s * GROUP + r) * rows, rows)
                out[:, where] = out[:, where] + far_in[s, r].T / samples

    for k in (1, 2, 3):
        for h in (0, 1):
            swap(k, h).wait_send()
    for d in range(1, planes):
        sum_copy(z, d).wait_send()

    def drain(t, carry):
        plane, r = t // GROUP, t % GROUP

        @pl.when((z > 0) & (plane >= z))
        def _():
            left(plane, r, other.at[plane, r]).wait_send()

        @pl.when((z < planes - 1) & (plane <= z))
        def _():
            right(plane, r, other.at[plane, r]).wait_send()

        for j in range(2):
            core_copy(plane, r, j).wait_send()
        y_copy(plane, r).wait_send()

        @pl.when(r // 2 != x)
        def _():
            x_copy(plane, r).wait_send()

        @pl.when((r // 2 == x) & (plane // per != x))
        def _():
            near_copy(plane, r).wait_send()

        @pl.when((r // 2 == x) & (plane != z))
        def _():
            far_copy(plane, r).wait_send()

        return carry

    lax.fori_loop(0, steps, drain, 0)


def lines(jacobian):
    rows, total = jacobian.shape
    count = lax.axis_size("samp")
    planes = count // GROUP
    per = planes // 2
    width = total // GROUP
    half = width // 2
    f32 = jnp.float32
    dma = pltpu.SemaphoreType.DMA
    body = functools.partial(kernel, planes, rows, width, float(rows * count))
    return pl.pallas_call(
        body,
        out_shape=jax.ShapeDtypeStruct((rows, per * GROUP * rows), f32),
        in_specs=[pl.BlockSpec(memory_space=pl.ANY)],
        out_specs=pl.BlockSpec(memory_space=pltpu.VMEM),
        scratch_shapes=[
            pltpu.VMEM((2, GROUP, rows, half), f32),
            pltpu.VMEM((2, GROUP, rows, half), jnp.bfloat16),
            pltpu.VMEM((2, GROUP, rows, half), jnp.bfloat16),
            pltpu.VMEM((planes, GROUP, rows, half), f32),
            pltpu.VMEM((planes, 2, 8, half), f32),
            pltpu.VMEM((2, 1, half), f32),
            pltpu.VMEM((planes, GROUP, GROUP, rows, rows), f32),
            pltpu.VMEM((planes, GROUP, 2, rows, rows), f32),
            pltpu.VMEM((planes, GROUP, rows, rows), f32),
            pltpu.VMEM((planes, 2, rows, rows), f32),
            pltpu.VMEM((per, 2, rows, rows), f32),
            pltpu.VMEM((per, GROUP, rows, rows), f32),
            dma((2,)),
            dma((GROUP, 2)), dma((GROUP, 2)),
            dma((planes,)), dma((planes,)),
            dma((2, planes, GROUP)), dma((planes, GROUP)),
            dma((planes, GROUP, 2)), dma((planes, GROUP, 2)),
            dma((planes, GROUP)), dma((planes, GROUP)),
            dma((planes, GROUP)), dma((planes, GROUP)),
            dma((planes, GROUP)), dma((per, 2)),
            dma((planes, GROUP)), dma((per, GROUP)),
        ],
        compiler_params=pltpu.CompilerParams(
            collective_id=0, has_side_effects=True, vmem_limit_bytes=60 * 2**20
        ),
    )(jacobian)


def tile_product(a, b):
    return jnp.dot(a, b.T, preferred_element_type=jnp.float32, precision=lax.Precision.HIGHEST)


def gathered(jacobian):
    rows = jacobian.shape[0]
    samples = rows * lax.axis_size("samp")
    totals = lax.psum(jnp.sum(jacobian, axis=0), "samp")
    centred = jacobian - (totals / samples)[None, :]
    partial_rows = tile_product(centred, lax.all_gather(centred, "samp", axis=0, tiled=True))
    return lax.psum_scatter(partial_rows, "par", scatter_dimension=1, tiled=True) / samples


def scratch_bytes(rows, total, planes):
    square = rows * rows * 4
    return rows * total * 4 * 2 + planes * rows * total * 2 + planes * square * 30 + planes * square * 5


def solution(mesh):
    planes, rest = divmod(mesh.shape["samp"], GROUP)

    def per_device(jacobian):
        rows, total = jacobian.shape
        fits = scratch_bytes(rows, total, planes) <= 56 * 2**20
        if mesh.shape["par"] == 2 and rest == 0 and planes % 2 == 0 and fits and total % 1024 == 0:
            return lines(jacobian)
        return gathered(jacobian)

    return jax.shard_map(
        per_device, mesh=mesh, in_specs=(P("samp", "par"),), out_specs=P("samp", "par"), check_vma=False
    )
```

```python
import functools

import jax
import jax.numpy as jnp
from jax import lax
from jax.experimental import pallas as pl
from jax.experimental.pallas import tpu as pltpu
from jax.sharding import PartitionSpec as P

MESH = pl.DeviceIdType.MESH
GROUP = 4


def split(value):
    high = value.astype(jnp.bfloat16)
    low = (value - high.astype(jnp.float32)).astype(jnp.bfloat16)
    return high, low


def product(a_high, a_low, b_high, b_low):
    dims = (((1,), (1,)), ((), ()))
    dot = functools.partial(lax.dot_general, dimension_numbers=dims, preferred_element_type=jnp.float32)
    return dot(a_high, b_high) + (dot(a_high, b_low) + dot(a_low, b_high))


def kernel(
    planes, rows, width, samples,
    jac, out,
    own, high, low, other, sums, mean, part, core_in, y_in, x_in, near_in, far_in,
    copy_sem, swap_send, swap_recv, sum_send, sum_recv, line_send, line_recv,
    core_send, core_recv, y_send, y_recv, x_send, x_recv,
    near_send, near_recv, far_send, far_recv,
):
    half = width // 2
    per = planes // 2
    samp = lax.axis_index("samp")
    x = lax.axis_index("par")
    z = samp // GROUP
    q = samp % GROUP
    devices = planes * GROUP * 2
    me = samp * 2 + x

    def flip(a, k):
        low_a, high_a = a % 2, a // 2
        low_k, high_k = k % 2, k // 2
        return (low_a + low_k) % 2 + 2 * ((high_a + high_k) % 2)

    def remote(src, dst, send, recv, to_samp, to_par):
        return pltpu.make_async_remote_copy(
            src_ref=src, dst_ref=dst, send_sem=send, recv_sem=recv,
            device_id=(to_samp, to_par), device_id_type=MESH,
        )

    barrier = pltpu.get_barrier_semaphore()

    def greet(i, carry):
        @pl.when(i != me)
        def _():
            pl.semaphore_signal(barrier, inc=1, device_id=(i // 2, i % 2), device_id_type=MESH)
        return carry

    lax.fori_loop(0, devices, greet, 0)
    pl.semaphore_wait(barrier, devices - 1)

    def columns(i, h):
        return pl.ds(pl.multiple_of(i * width + h * half, half), half)

    def swap(k, h):
        to = flip(q, k)
        return remote(
            jac.at[:, columns(to, h)], own.at[h, q], swap_send.at[k, h], swap_recv.at[q, h],
            z * GROUP + to, x,
        )

    def swap_in(k, h):
        source = flip(q, k)
        return remote(
            jac.at[:, columns(q, h)], own.at[h, source], swap_send.at[k, h],
            swap_recv.at[source, h], z * GROUP + source, x,
        )

    mine = [
        pltpu.make_async_copy(jac.at[:, columns(q, h)], own.at[h, q], copy_sem.at[h]) for h in (0, 1)
    ]
    def left(plane, r, src):
        return remote(
            src, other.at[plane, r], line_send.at[0, plane, r], line_recv.at[plane, r],
            (z - 1) * GROUP + q, x,
        )

    def right(plane, r, src):
        return remote(
            src, other.at[plane, r], line_send.at[1, plane, r], line_recv.at[plane, r],
            (z + 1) * GROUP + q, x,
        )

    def send_own(r, sources):
        @pl.when(z > 0)
        def _():
            left(z, r, sources[0]).start()

        @pl.when(z < planes - 1)
        def _():
            right(z, r, sources[1]).start()

    def send_swap(k):
        for h in (0, 1):
            swap(k, h).start()

    for h in (0, 1):
        mine[h].start()
    send_swap(1)
    send_own(q, [jac.at[:, columns(q, h)] for h in (0, 1)])
    send_swap(2)

    totals = [jnp.zeros((8, half), jnp.float32) for _ in range(2)]
    for k in range(GROUP):
        r = flip(q, k)
        for h in (0, 1):
            if k == 0:
                mine[h].wait()
            else:
                swap_in(k, h).wait_recv()

            if k > 0:
                @pl.when((z > 0) if h == 0 else (z < planes - 1))
                def _():
                    (left if h == 0 else right)(z, r, own.at[h, r]).start()

        if k == 1:
            send_swap(3)
        for h in (0, 1):
            def add(i, acc):
                return acc + own[h, r, pl.ds(pl.multiple_of(i * 8, 8), 8), :]

            totals[h] = lax.fori_loop(0, rows // 8, add, totals[h])
    for h in (0, 1):
        sums[z, h] = totals[h]

    def sum_copy(plane, d):
        to = lax.rem(z + d, planes)
        return remote(
            sums.at[plane], sums.at[plane], sum_send.at[d], sum_recv.at[plane], to * GROUP + q, x
        )

    for d in range(1, planes):
        sum_copy(z, d).start()

    def relay(d, r, passes):
        before, after = z - d, z + d

        @pl.when((after < planes) & ((z > 0) == passes))
        def _():
            left(after, r, other.at[after, r]).wait_recv()
            if passes:
                left(after, r, other.at[after, r]).start()

        @pl.when((before >= 0) & ((z < planes - 1) == passes))
        def _():
            right(before, r, other.at[before, r]).wait_recv()
            if passes:
                right(before, r, other.at[before, r]).start()

    for r in range(GROUP):
        relay(1, r, True)

    for d in range(1, planes):
        sum_copy(lax.rem(z + d, planes), d).wait_recv()
    for h in (0, 1):
        whole = sums[0, h]
        for d in range(1, planes):
            whole = whole + sums[d, h]
        mean[h] = jnp.sum(whole, axis=0, keepdims=True) / samples

    @pl.loop(0, GROUP)
    def _(i):
        for h in (0, 1):
            a, b = split(own[h, i] - mean[h])
            high[h, i] = a
            low[h, i] = b

    def square(r):
        @pl.loop(0, GROUP)
        def _(i):
            part[z, i, r] = product(high[0, i], low[0, i], high[0, r], low[0, r]) + product(
                high[1, i], low[1, i], high[1, r], low[1, r]
            )

    def multiply(plane, r, h):
        b_high, b_low = split(other[plane, r] - mean[h])

        @pl.loop(0, GROUP)
        def _(i):
            part[plane, i, r] = product(high[h, i], low[h, i], b_high, b_low)

    def core_copy(plane, r, j):
        block = flip(q, 1 + 2 * j)
        return remote(
            part.at[plane, block, r], core_in.at[plane, r, j], core_send.at[plane, r, j],
            core_recv.at[plane, r, j], z * GROUP + flip(q, 1), x,
        )

    def y_copy(plane, r):
        return remote(
            part.at[plane, flip(q, 2), r], y_in.at[plane, r], y_send.at[plane, r],
            y_recv.at[plane, r], z * GROUP + flip(q, 2), x,
        )

    def x_copy(plane, r):
        return remote(
            part.at[plane, q, r], x_in.at[plane, r % 2], x_send.at[plane, r],
            x_recv.at[plane, r], samp, 1 - x,
        )

    def near_copy(plane, r):
        return remote(
            part.at[plane, q, r], near_in.at[plane % per, r % 2], near_send.at[plane, r],
            near_recv.at[plane % per, r % 2], samp, 1 - x,
        )

    def far_copy(plane, r):
        return remote(
            part.at[plane, q, r], far_in.at[z % per, q], far_send.at[plane, r],
            far_recv.at[z % per, q], plane * GROUP + r, z // per,
        )

    def stage0(plane, r):
        for j in (1, 0):
            core_copy(plane, r, j).start()

    def stage1(plane, r):
        core_copy(plane, r, 1).wait_recv()
        block = flip(q, 2)
        part[plane, block, r] = part[plane, block, r] + core_in[plane, r, 1]
        y_copy(plane, r).start()
        core_copy(plane, r, 0).wait_recv()
        part[plane, q, r] = part[plane, q, r] + core_in[plane, r, 0]

    def stage2(plane, r):
        y_copy(plane, r).wait_recv()
        part[plane, q, r] = part[plane, q, r] + y_in[plane, r]

        @pl.when(r // 2 != x)
        def _():
            x_copy(plane, r).start()

    def stage3(plane, r):
        @pl.when(r // 2 == x)
        def _():
            x_copy(plane, r).wait_recv()
            part[plane, q, r] = part[plane, q, r] + x_in[plane, r % 2]

            @pl.when(plane // per != x)
            def _():
                near_copy(plane, r).start()

            @pl.when(plane != z)
            def _():
                far_copy(plane, r).start()

    steps = planes * GROUP

    def each(e, run):
        d, r = e // GROUP, e % GROUP

        @pl.when((e >= 0) & (e < steps) & (z + d < planes))
        def _():
            run(z + d, r)

        @pl.when((e >= GROUP) & (e < steps) & (z - d >= 0))
        def _():
            run(z - d, r)

    def step(e, carry):
        d, r = e // GROUP, e % GROUP
        @pl.when((d > 0) & (d + 1 < planes))
        def _():
            relay(d + 1, r, True)

        each(e - 5, stage3)
        each(e - 3, stage2)

        @pl.when(e > 2 * GROUP)
        def _():
            each(e - 1, stage1)

        @pl.when((d > 0) & (d < planes))
        def _():
            relay(d, r, False)

        @pl.when(d == 0)
        def _():
            square(r)

        @pl.when((d > 0) & (z + d < planes))
        def _():
            multiply(z + d, r, 0)

        @pl.when((d > 0) & (z - d >= 0))
        def _():
            multiply(z - d, r, 1)

        each(e, stage0)

        @pl.when(e <= 2 * GROUP)
        def _():
            each(e - 1, stage1)

        return carry

    lax.fori_loop(0, steps + 5, step, 0)

    for s in range(per):
        plane = x * per + s
        for j in range(2):
            near_copy(plane, j).wait_recv()
        for r in range(GROUP):
            kept = part[plane, q, r]
            sent = near_in[s, r % 2]
            where = pl.ds((s * GROUP + r) * rows, rows)
            out[:, where] = jnp.where(x == r // 2, kept, sent) / samples

        @pl.when(plane != z)
        def _():
            for r in range(GROUP):
                remote(
                    part.at[plane, q, r], far_in.at[s, r], far_send.at[plane, r], far_recv.at[s, r],
                    samp, 1 - x,
                ).wait_recv()
                where = pl.ds((s * GROUP + r) * rows, rows)
                out[:, where] = out[:, where] + far_in[s, r].T / samples

    for k in (1, 2, 3):
        for h in (0, 1):
            swap(k, h).wait_send()
    for d in range(1, planes):
        sum_copy(z, d).wait_send()

    def drain(t, carry):
        plane, r = t // GROUP, t % GROUP

        @pl.when((z > 0) & (plane >= z))
        def _():
            left(plane, r, other.at[plane, r]).wait_send()

        @pl.when((z < planes - 1) & (plane <= z))
        def _():
            right(plane, r, other.at[plane, r]).wait_send()

        for j in range(2):
            core_copy(plane, r, j).wait_send()
        y_copy(plane, r).wait_send()

        @pl.when(r // 2 != x)
        def _():
            x_copy(plane, r).wait_send()

        @pl.when((r // 2 == x) & (plane // per != x))
        def _():
            near_copy(plane, r).wait_send()

        @pl.when((r // 2 == x) & (plane != z))
        def _():
            far_copy(plane, r).wait_send()

        return carry

    lax.fori_loop(0, steps, drain, 0)


def lines(jacobian):
    rows, total = jacobian.shape
    count = lax.axis_size("samp")
    planes = count // GROUP
    per = planes // 2
    width = total // GROUP
    half = width // 2
    f32 = jnp.float32
    dma = pltpu.SemaphoreType.DMA
    body = functools.partial(kernel, planes, rows, width, float(rows * count))
    return pl.pallas_call(
        body,
        out_shape=jax.ShapeDtypeStruct((rows, per * GROUP * rows), f32),
        in_specs=[pl.BlockSpec(memory_space=pl.ANY)],
        out_specs=pl.BlockSpec(memory_space=pltpu.VMEM),
        scratch_shapes=[
            pltpu.VMEM((2, GROUP, rows, half), f32),
            pltpu.VMEM((2, GROUP, rows, half), jnp.bfloat16),
            pltpu.VMEM((2, GROUP, rows, half), jnp.bfloat16),
            pltpu.VMEM((planes, GROUP, rows, half), f32),
            pltpu.VMEM((planes, 2, 8, half), f32),
            pltpu.VMEM((2, 1, half), f32),
            pltpu.VMEM((planes, GROUP, GROUP, rows, rows), f32),
            pltpu.VMEM((planes, GROUP, 2, rows, rows), f32),
            pltpu.VMEM((planes, GROUP, rows, rows), f32),
            pltpu.VMEM((planes, 2, rows, rows), f32),
            pltpu.VMEM((per, 2, rows, rows), f32),
            pltpu.VMEM((per, GROUP, rows, rows), f32),
            dma((2,)),
            dma((GROUP, 2)), dma((GROUP, 2)),
            dma((planes,)), dma((planes,)),
            dma((2, planes, GROUP)), dma((planes, GROUP)),
            dma((planes, GROUP, 2)), dma((planes, GROUP, 2)),
            dma((planes, GROUP)), dma((planes, GROUP)),
            dma((planes, GROUP)), dma((planes, GROUP)),
            dma((planes, GROUP)), dma((per, 2)),
            dma((planes, GROUP)), dma((per, GROUP)),
        ],
        compiler_params=pltpu.CompilerParams(
            collective_id=0, has_side_effects=True, vmem_limit_bytes=60 * 2**20
        ),
    )(jacobian)


def tile_product(a, b):
    return jnp.dot(a, b.T, preferred_element_type=jnp.float32, precision=lax.Precision.HIGHEST)


def gathered(jacobian):
    rows = jacobian.shape[0]
    samples = rows * lax.axis_size("samp")
    totals = lax.psum(jnp.sum(jacobian, axis=0), "samp")
    centred = jacobian - (totals / samples)[None, :]
    partial_rows = tile_product(centred, lax.all_gather(centred, "samp", axis=0, tiled=True))
    return lax.psum_scatter(partial_rows, "par", scatter_dimension=1, tiled=True) / samples


def scratch_bytes(rows, total, planes):
    square = rows * rows * 4
    return rows * total * 4 * 2 + planes * rows * total * 2 + planes * square * 30 + planes * square * 5


def solution(mesh):
    planes, rest = divmod(mesh.shape["samp"], GROUP)

    def per_device(jacobian):
        rows, total = jacobian.shape
        fits = scratch_bytes(rows, total, planes) <= 56 * 2**20
        if mesh.shape["par"] == 2 and rest == 0 and planes % 2 == 0 and fits and total % 1024 == 0:
            return lines(jacobian)
        return gathered(jacobian)

    return jax.shard_map(
        per_device, mesh=mesh, in_specs=(P("samp", "par"),), out_specs=P("samp", "par"), check_vma=False
    )
```

```python
import functools

import jax
import jax.numpy as jnp
from jax import lax
from jax.experimental import pallas as pl
from jax.experimental.pallas import tpu as pltpu
from jax.sharding import PartitionSpec as P

MESH = pl.DeviceIdType.MESH
GROUP = 4


def split(value):
    high = value.astype(jnp.bfloat16)
    low = (value - high.astype(jnp.float32)).astype(jnp.bfloat16)
    return high, low


def product(a_high, a_low, b_high, b_low):
    dims = (((1,), (1,)), ((), ()))
    dot = functools.partial(lax.dot_general, dimension_numbers=dims, preferred_element_type=jnp.float32)
    return dot(a_high, b_high) + (dot(a_high, b_low) + dot(a_low, b_high))


def kernel(
    planes, rows, width, samples,
    jac, out,
    own, high, low, other, sums, mean, part, core_in, y_in, x_in, near_in, far_in,
    copy_sem, swap_send, swap_recv, sum_send, sum_recv, line_send, line_recv,
    core_send, core_recv, y_send, y_recv, x_send, x_recv,
    near_send, near_recv, far_send, far_recv,
):
    half = width // 2
    per = planes // 2
    samp = lax.axis_index("samp")
    x = lax.axis_index("par")
    z = samp // GROUP
    q = samp % GROUP
    devices = planes * GROUP * 2
    me = samp * 2 + x

    def flip(a, k):
        low_a, high_a = a % 2, a // 2
        low_k, high_k = k % 2, k // 2
        return (low_a + low_k) % 2 + 2 * ((high_a + high_k) % 2)

    def remote(src, dst, send, recv, to_samp, to_par):
        return pltpu.make_async_remote_copy(
            src_ref=src, dst_ref=dst, send_sem=send, recv_sem=recv,
            device_id=(to_samp, to_par), device_id_type=MESH,
        )

    barrier = pltpu.get_barrier_semaphore()

    def greet(i, carry):
        @pl.when(i != me)
        def _():
            pl.semaphore_signal(barrier, inc=1, device_id=(i // 2, i % 2), device_id_type=MESH)
        return carry

    lax.fori_loop(0, devices, greet, 0)
    pl.semaphore_wait(barrier, devices - 1)

    def columns(i, h):
        return pl.ds(pl.multiple_of(i * width + h * half, half), half)

    def swap(k, h):
        to = flip(q, k)
        return remote(
            jac.at[:, columns(to, h)], own.at[h, q], swap_send.at[k, h], swap_recv.at[q, h],
            z * GROUP + to, x,
        )

    def swap_in(k, h):
        source = flip(q, k)
        return remote(
            jac.at[:, columns(q, h)], own.at[h, source], swap_send.at[k, h],
            swap_recv.at[source, h], z * GROUP + source, x,
        )

    mine = [
        pltpu.make_async_copy(jac.at[:, columns(q, h)], own.at[h, q], copy_sem.at[h]) for h in (0, 1)
    ]
    def left(plane, r, src):
        return remote(
            src, other.at[plane, r], line_send.at[0, plane, r], line_recv.at[plane, r],
            (z - 1) * GROUP + q, x,
        )

    def right(plane, r, src):
        return remote(
            src, other.at[plane, r], line_send.at[1, plane, r], line_recv.at[plane, r],
            (z + 1) * GROUP + q, x,
        )

    def send_own(r, sources):
        @pl.when(z > 0)
        def _():
            left(z, r, sources[0]).start()

        @pl.when(z < planes - 1)
        def _():
            right(z, r, sources[1]).start()

    def send_swap(k):
        for h in (0, 1):
            swap(k, h).start()

    for h in (0, 1):
        mine[h].start()
    send_swap(1)
    send_own(q, [jac.at[:, columns(q, h)] for h in (0, 1)])
    send_swap(2)

    totals = [jnp.zeros((8, half), jnp.float32) for _ in range(2)]
    for k in range(GROUP):
        r = flip(q, k)
        for h in (0, 1):
            if k == 0:
                mine[h].wait()
            else:
                swap_in(k, h).wait_recv()

            if k > 0:
                @pl.when((z > 0) if h == 0 else (z < planes - 1))
                def _():
                    (left if h == 0 else right)(z, r, own.at[h, r]).start()

        if k == 1:
            send_swap(3)
        for h in (0, 1):
            def add(i, acc):
                return acc + own[h, r, pl.ds(pl.multiple_of(i * 8, 8), 8), :]

            totals[h] = lax.fori_loop(0, rows // 8, add, totals[h])
    for h in (0, 1):
        sums[z, h] = totals[h]

    def sum_copy(plane, d):
        to = lax.rem(z + d, planes)
        return remote(
            sums.at[plane], sums.at[plane], sum_send.at[d], sum_recv.at[plane], to * GROUP + q, x
        )

    for d in range(1, planes):
        sum_copy(z, d).start()

    def relay(d, r, passes):
        before, after = z - d, z + d

        @pl.when((after < planes) & ((z > 0) == passes))
        def _():
            left(after, r, other.at[after, r]).wait_recv()
            if passes:
                left(after, r, other.at[after, r]).start()

        @pl.when((before >= 0) & ((z < planes - 1) == passes))
        def _():
            right(before, r, other.at[before, r]).wait_recv()
            if passes:
                right(before, r, other.at[before, r]).start()

    for r in range(GROUP):
        relay(1, r, True)

    for d in range(1, planes):
        sum_copy(lax.rem(z + d, planes), d).wait_recv()
    for h in (0, 1):
        whole = sums[0, h]
        for d in range(1, planes):
            whole = whole + sums[d, h]
        mean[h] = jnp.sum(whole, axis=0, keepdims=True) / samples

    @pl.loop(0, GROUP)
    def _(i):
        for h in (0, 1):
            a, b = split(own[h, i] - mean[h])
            high[h, i] = a
            low[h, i] = b

    def square(r):
        @pl.loop(0, GROUP)
        def _(i):
            part[z, i, r] = product(high[0, i], low[0, i], high[0, r], low[0, r]) + product(
                high[1, i], low[1, i], high[1, r], low[1, r]
            )

    def multiply(plane, r, h):
        b_high, b_low = split(other[plane, r] - mean[h])

        @pl.loop(0, GROUP)
        def _(i):
            part[plane, i, r] = product(high[h, i], low[h, i], b_high, b_low)

    def core_copy(plane, r, j):
        block = flip(q, 1 + 2 * j)
        return remote(
            part.at[plane, block, r], core_in.at[plane, r, j], core_send.at[plane, r, j],
            core_recv.at[plane, r, j], z * GROUP + flip(q, 1), x,
        )

    def y_copy(plane, r):
        return remote(
            part.at[plane, flip(q, 2), r], y_in.at[plane, r], y_send.at[plane, r],
            y_recv.at[plane, r], z * GROUP + flip(q, 2), x,
        )

    def x_copy(plane, r, j):
        return remote(
            part.at[plane, flip(q, 2 * j), r], x_in.at[plane, r % 2 + j], x_send.at[plane, r, j],
            x_recv.at[plane, r, j], samp, 1 - x,
        )

    def near_copy(plane, r):
        return remote(
            part.at[plane, q, r], near_in.at[plane % per, r % 2], near_send.at[plane, r],
            near_recv.at[plane % per, r % 2], samp, 1 - x,
        )

    def far_copy(plane, r):
        return remote(
            part.at[plane, q, r], far_in.at[z % per, q], far_send.at[plane, r],
            far_recv.at[z % per, q], plane * GROUP + r, z // per,
        )

    def stage0(plane, r):
        for j in (1, 0):
            core_copy(plane, r, j).start()

    def add_y(plane, r):
        y_copy(plane, r).wait_recv()
        part[plane, q, r] = part[plane, q, r] + y_in[plane, r]

    def add_x(plane, r, j):
        x_copy(plane, r, j).wait_recv()
        block = flip(q, 2 * j)
        part[plane, block, r] = part[plane, block, r] + x_in[plane, r % 2 + j]

    def stage1(plane, r):
        core_copy(plane, r, 1).wait_recv()
        block = flip(q, 2)
        part[plane, block, r] = part[plane, block, r] + core_in[plane, r, 1]

        @pl.when(r % 2 == 0)
        def _():
            y_copy(plane, r).start()

        @pl.when((r % 2 == 1) & (r // 2 != x))
        def _():
            x_copy(plane, r, 1).start()

        core_copy(plane, r, 0).wait_recv()
        part[plane, q, r] = part[plane, q, r] + core_in[plane, r, 0]

        @pl.when((r % 2 == 1) & (r // 2 != x))
        def _():
            x_copy(plane, r, 0).start()

    def stage2(plane, r):
        @pl.when(r % 2 == 0)
        def _():
            add_y(plane, r)

            @pl.when(r // 2 != x)
            def _():
                x_copy(plane, r, 0).start()

        @pl.when((r % 2 == 1) & (r // 2 == x))
        def _():
            add_x(plane, r, 1)
            y_copy(plane, r).start()
            add_x(plane, r, 0)

    def stage3(plane, r):
        @pl.when(r // 2 == x)
        def _():
            @pl.when(r % 2 == 0)
            def _():
                add_x(plane, r, 0)

            @pl.when(r % 2 == 1)
            def _():
                add_y(plane, r)

            @pl.when(plane // per != x)
            def _():
                near_copy(plane, r).start()

            @pl.when(plane != z)
            def _():
                far_copy(plane, r).start()

    steps = planes * GROUP

    def each(e, run):
        d, r = e // GROUP, e % GROUP

        @pl.when((e >= 0) & (e < steps) & (z + d < planes))
        def _():
            run(z + d, r)

        @pl.when((e >= GROUP) & (e < steps) & (z - d >= 0))
        def _():
            run(z - d, r)

    def step(e, carry):
        d, r = e // GROUP, e % GROUP
        @pl.when((d > 0) & (d + 1 < planes))
        def _():
            relay(d + 1, r, True)

        each(e - 5, stage3)
        each(e - 3, stage2)

        @pl.when(e > 2 * GROUP)
        def _():
            each(e - 1, stage1)

        @pl.when((d > 0) & (d < planes))
        def _():
            relay(d, r, False)

        @pl.when(d == 0)
        def _():
            square(r)

        @pl.when((d > 0) & (z + d < planes))
        def _():
            multiply(z + d, r, 0)

        @pl.when((d > 0) & (z - d >= 0))
        def _():
            multiply(z - d, r, 1)

        each(e, stage0)

        @pl.when(e <= 2 * GROUP)
        def _():
            each(e - 1, stage1)

        return carry

    lax.fori_loop(0, steps + 5, step, 0)

    for s in range(per):
        plane = x * per + s
        for j in range(2):
            near_copy(plane, j).wait_recv()
        for r in range(GROUP):
            kept = part[plane, q, r]
            sent = near_in[s, r % 2]
            where = pl.ds((s * GROUP + r) * rows, rows)
            out[:, where] = jnp.where(x == r // 2, kept, sent) / samples

        @pl.when(plane != z)
        def _():
            for r in range(GROUP):
                remote(
                    part.at[plane, q, r], far_in.at[s, r], far_send.at[plane, r], far_recv.at[s, r],
                    samp, 1 - x,
                ).wait_recv()
                where = pl.ds((s * GROUP + r) * rows, rows)
                out[:, where] = out[:, where] + far_in[s, r].T / samples

    for k in (1, 2, 3):
        for h in (0, 1):
            swap(k, h).wait_send()
    for d in range(1, planes):
        sum_copy(z, d).wait_send()

    def drain(t, carry):
        plane, r = t // GROUP, t % GROUP

        @pl.when((z > 0) & (plane >= z))
        def _():
            left(plane, r, other.at[plane, r]).wait_send()

        @pl.when((z < planes - 1) & (plane <= z))
        def _():
            right(plane, r, other.at[plane, r]).wait_send()

        for j in range(2):
            core_copy(plane, r, j).wait_send()

        @pl.when((r % 2 == 0) | (r // 2 == x))
        def _():
            y_copy(plane, r).wait_send()

        @pl.when(r // 2 != x)
        def _():
            x_copy(plane, r, 0).wait_send()

            @pl.when(r % 2 == 1)
            def _():
                x_copy(plane, r, 1).wait_send()

        @pl.when((r // 2 == x) & (plane // per != x))
        def _():
            near_copy(plane, r).wait_send()

        @pl.when((r // 2 == x) & (plane != z))
        def _():
            far_copy(plane, r).wait_send()

        return carry

    lax.fori_loop(0, steps, drain, 0)


def lines(jacobian):
    rows, total = jacobian.shape
    count = lax.axis_size("samp")
    planes = count // GROUP
    per = planes // 2
    width = total // GROUP
    half = width // 2
    f32 = jnp.float32
    dma = pltpu.SemaphoreType.DMA
    body = functools.partial(kernel, planes, rows, width, float(rows * count))
    return pl.pallas_call(
        body,
        out_shape=jax.ShapeDtypeStruct((rows, per * GROUP * rows), f32),
        in_specs=[pl.BlockSpec(memory_space=pl.ANY)],
        out_specs=pl.BlockSpec(memory_space=pltpu.VMEM),
        scratch_shapes=[
            pltpu.VMEM((2, GROUP, rows, half), f32),
            pltpu.VMEM((2, GROUP, rows, half), jnp.bfloat16),
            pltpu.VMEM((2, GROUP, rows, half), jnp.bfloat16),
            pltpu.VMEM((planes, GROUP, rows, half), f32),
            pltpu.VMEM((planes, 2, 8, half), f32),
            pltpu.VMEM((2, 1, half), f32),
            pltpu.VMEM((planes, GROUP, GROUP, rows, rows), f32),
            pltpu.VMEM((planes, GROUP, 2, rows, rows), f32),
            pltpu.VMEM((planes, GROUP, rows, rows), f32),
            pltpu.VMEM((planes, 3, rows, rows), f32),
            pltpu.VMEM((per, 2, rows, rows), f32),
            pltpu.VMEM((per, GROUP, rows, rows), f32),
            dma((2,)),
            dma((GROUP, 2)), dma((GROUP, 2)),
            dma((planes,)), dma((planes,)),
            dma((2, planes, GROUP)), dma((planes, GROUP)),
            dma((planes, GROUP, 2)), dma((planes, GROUP, 2)),
            dma((planes, GROUP)), dma((planes, GROUP)),
            dma((planes, GROUP, 2)), dma((planes, GROUP, 2)),
            dma((planes, GROUP)), dma((per, 2)),
            dma((planes, GROUP)), dma((per, GROUP)),
        ],
        compiler_params=pltpu.CompilerParams(
            collective_id=0, has_side_effects=True, vmem_limit_bytes=60 * 2**20
        ),
    )(jacobian)


def tile_product(a, b):
    return jnp.dot(a, b.T, preferred_element_type=jnp.float32, precision=lax.Precision.HIGHEST)


def gathered(jacobian):
    rows = jacobian.shape[0]
    samples = rows * lax.axis_size("samp")
    totals = lax.psum(jnp.sum(jacobian, axis=0), "samp")
    centred = jacobian - (totals / samples)[None, :]
    partial_rows = tile_product(centred, lax.all_gather(centred, "samp", axis=0, tiled=True))
    return lax.psum_scatter(partial_rows, "par", scatter_dimension=1, tiled=True) / samples


def scratch_bytes(rows, total, planes):
    square = rows * rows * 4
    return rows * total * 4 * 2 + planes * rows * total * 2 + planes * square * 30 + planes * square * 5


def solution(mesh):
    planes, rest = divmod(mesh.shape["samp"], GROUP)

    def per_device(jacobian):
        rows, total = jacobian.shape
        fits = scratch_bytes(rows, total, planes) <= 56 * 2**20
        if mesh.shape["par"] == 2 and rest == 0 and planes % 2 == 0 and fits and total % 1024 == 0:
            return lines(jacobian)
        return gathered(jacobian)

    return jax.shard_map(
        per_device, mesh=mesh, in_specs=(P("samp", "par"),), out_specs=P("samp", "par"), check_vma=False
    )
```

```python
import functools

import jax
import jax.numpy as jnp
from jax import lax
from jax.experimental import pallas as pl
from jax.experimental.pallas import tpu as pltpu
from jax.sharding import PartitionSpec as P

MESH = pl.DeviceIdType.MESH
GROUP = 4


def split(value):
    high = value.astype(jnp.bfloat16)
    low = (value - high.astype(jnp.float32)).astype(jnp.bfloat16)
    return high, low


def product(a_high, a_low, b_high, b_low):
    dims = (((1,), (1,)), ((), ()))
    dot = functools.partial(lax.dot_general, dimension_numbers=dims, preferred_element_type=jnp.float32)
    return dot(a_high, b_high) + (dot(a_high, b_low) + dot(a_low, b_high))


def kernel(
    planes, rows, width, samples,
    jac, out,
    own, high, low, other, sums, mean, part, core_in, y_in, x_in, near_in, far_in,
    copy_sem, swap_send, swap_recv, sum_send, sum_recv, line_send, line_recv,
    core_send, core_recv, y_send, y_recv, x_send, x_recv,
    near_send, near_recv, far_send, far_recv,
):
    half = width // 2
    per = planes // 2
    samp = lax.axis_index("samp")
    x = lax.axis_index("par")
    z = samp // GROUP
    q = samp % GROUP
    devices = planes * GROUP * 2
    me = samp * 2 + x

    def flip(a, k):
        low_a, high_a = a % 2, a // 2
        low_k, high_k = k % 2, k // 2
        return (low_a + low_k) % 2 + 2 * ((high_a + high_k) % 2)

    def remote(src, dst, send, recv, to_samp, to_par):
        return pltpu.make_async_remote_copy(
            src_ref=src, dst_ref=dst, send_sem=send, recv_sem=recv,
            device_id=(to_samp, to_par), device_id_type=MESH,
        )

    barrier = pltpu.get_barrier_semaphore()

    def greet(i, carry):
        @pl.when(i != me)
        def _():
            pl.semaphore_signal(barrier, inc=1, device_id=(i // 2, i % 2), device_id_type=MESH)
        return carry

    lax.fori_loop(0, devices, greet, 0)
    pl.semaphore_wait(barrier, devices - 1)

    def columns(i, h):
        return pl.ds(pl.multiple_of(i * width + h * half, half), half)

    def swap(k, h):
        to = flip(q, k)
        return remote(
            jac.at[:, columns(to, h)], own.at[h, q], swap_send.at[k, h], swap_recv.at[q, h],
            z * GROUP + to, x,
        )

    def swap_in(k, h):
        source = flip(q, k)
        return remote(
            jac.at[:, columns(q, h)], own.at[h, source], swap_send.at[k, h],
            swap_recv.at[source, h], z * GROUP + source, x,
        )

    mine = [
        pltpu.make_async_copy(jac.at[:, columns(q, h)], own.at[h, q], copy_sem.at[h]) for h in (0, 1)
    ]
    def left(plane, r, src):
        return remote(
            src, other.at[plane, r], line_send.at[0, plane, r], line_recv.at[plane, r],
            (z - 1) * GROUP + q, x,
        )

    def right(plane, r, src):
        return remote(
            src, other.at[plane, r], line_send.at[1, plane, r], line_recv.at[plane, r],
            (z + 1) * GROUP + q, x,
        )

    def send_own(r, sources):
        @pl.when(z > 0)
        def _():
            left(z, r, sources[0]).start()

        @pl.when(z < planes - 1)
        def _():
            right(z, r, sources[1]).start()

    def send_swap(k):
        for h in (0, 1):
            swap(k, h).start()

    for h in (0, 1):
        mine[h].start()
    send_swap(1)
    send_own(q, [jac.at[:, columns(q, h)] for h in (0, 1)])
    send_swap(2)

    totals = [jnp.zeros((8, half), jnp.float32) for _ in range(2)]
    for k in range(GROUP):
        r = flip(q, k)
        for h in (0, 1):
            if k == 0:
                mine[h].wait()
            else:
                swap_in(k, h).wait_recv()

            if k > 0:
                @pl.when((z > 0) if h == 0 else (z < planes - 1))
                def _():
                    (left if h == 0 else right)(z, r, own.at[h, r]).start()

        if k == 1:
            send_swap(3)
        for h in (0, 1):
            def add(i, acc):
                return acc + own[h, r, pl.ds(pl.multiple_of(i * 8, 8), 8), :]

            totals[h] = lax.fori_loop(0, rows // 8, add, totals[h])
    for h in (0, 1):
        sums[z, h] = totals[h]

    def sum_copy(plane, d):
        to = lax.rem(z + d, planes)
        return remote(
            sums.at[plane], sums.at[plane], sum_send.at[d], sum_recv.at[plane], to * GROUP + q, x
        )

    for d in range(1, planes):
        sum_copy(z, d).start()

    def relay(d, r, passes):
        before, after = z - d, z + d

        @pl.when((after < planes) & ((z > 0) == passes))
        def _():
            left(after, r, other.at[after, r]).wait_recv()
            if passes:
                left(after, r, other.at[after, r]).start()

        @pl.when((before >= 0) & ((z < planes - 1) == passes))
        def _():
            right(before, r, other.at[before, r]).wait_recv()
            if passes:
                right(before, r, other.at[before, r]).start()

    for r in range(GROUP):
        relay(1, r, True)

    for d in range(1, planes):
        sum_copy(lax.rem(z + d, planes), d).wait_recv()
    for h in (0, 1):
        whole = sums[0, h]
        for d in range(1, planes):
            whole = whole + sums[d, h]
        mean[h] = jnp.sum(whole, axis=0, keepdims=True) / samples

    @pl.loop(0, GROUP)
    def _(i):
        for h in (0, 1):
            a, b = split(own[h, i] - mean[h])
            high[h, i] = a
            low[h, i] = b

    def square(r):
        @pl.loop(0, GROUP)
        def _(i):
            part[z, i, r] = product(high[0, i], low[0, i], high[0, r], low[0, r]) + product(
                high[1, i], low[1, i], high[1, r], low[1, r]
            )

    def multiply(plane, r, h):
        b_high, b_low = split(other[plane, r] - mean[h])

        @pl.loop(0, GROUP)
        def _(i):
            part[plane, i, r] = product(high[h, i], low[h, i], b_high, b_low)

    def core_copy(plane, r, j):
        block = flip(q, 1 + 2 * j)
        return remote(
            part.at[plane, block, r], core_in.at[plane, r, j], core_send.at[plane, r, j],
            core_recv.at[plane, r, j], z * GROUP + flip(q, 1), x,
        )

    def y_copy(plane, r):
        return remote(
            part.at[plane, flip(q, 2), r], y_in.at[plane, r], y_send.at[plane, r],
            y_recv.at[plane, r], z * GROUP + flip(q, 2), x,
        )

    def x_copy(plane, r):
        return remote(
            part.at[plane, q, r], x_in.at[plane, r % 2], x_send.at[plane, r],
            x_recv.at[plane, r], samp, 1 - x,
        )

    def near_copy(plane, r):
        return remote(
            part.at[plane, q, r], near_in.at[plane % per, r % 2], near_send.at[plane, r],
            near_recv.at[plane % per, r % 2], samp, 1 - x,
        )

    def far_copy(plane, r):
        return remote(
            part.at[plane, q, r], far_in.at[z % per, q], far_send.at[plane, r],
            far_recv.at[z % per, q], plane * GROUP + r, z // per,
        )

    def stage0(plane, r):
        for j in (1, 0):
            core_copy(plane, r, j).start()

    def stage1(plane, r):
        core_copy(plane, r, 1).wait_recv()
        block = flip(q, 2)
        part[plane, block, r] = part[plane, block, r] + core_in[plane, r, 1]
        y_copy(plane, r).start()
        core_copy(plane, r, 0).wait_recv()
        part[plane, q, r] = part[plane, q, r] + core_in[plane, r, 0]

    def stage2(plane, r):
        y_copy(plane, r).wait_recv()
        part[plane, q, r] = part[plane, q, r] + y_in[plane, r]

        @pl.when(r // 2 != x)
        def _():
            x_copy(plane, r).start()

    def stage3(plane, r):
        @pl.when(r // 2 == x)
        def _():
            x_copy(plane, r).wait_recv()
            part[plane, q, r] = part[plane, q, r] + x_in[plane, r % 2]

            @pl.when(plane // per != x)
            def _():
                near_copy(plane, r).start()

            @pl.when(plane != z)
            def _():
                far_copy(plane, r).start()

    steps = planes * GROUP

    def each(e, run):
        d, r = e // GROUP, e % GROUP

        @pl.when((e >= 0) & (e < steps) & (z + d < planes))
        def _():
            run(z + d, r)

        @pl.when((e >= GROUP) & (e < steps) & (z - d >= 0))
        def _():
            run(z - d, r)

    def step(e, carry):
        d, r = e // GROUP, e % GROUP
        each(e - 5, stage3)
        each(e - 3, stage2)

        @pl.when(e > 2 * GROUP)
        def _():
            each(e - 1, stage1)

        @pl.when((d > 0) & (d < planes))
        def _():
            relay(d, r, False)

        @pl.when(d == 0)
        def _():
            square(r)

        @pl.when((d > 0) & (z + d < planes))
        def _():
            multiply(z + d, r, 0)

        @pl.when((d > 0) & (z - d >= 0))
        def _():
            multiply(z - d, r, 1)

        each(e, stage0)

        @pl.when((d > 0) & (d + 1 < planes))
        def _():
            relay(d + 1, r, True)

        @pl.when(e <= 2 * GROUP)
        def _():
            each(e - 1, stage1)

        return carry

    lax.fori_loop(0, steps + 5, step, 0)

    for s in range(per):
        plane = x * per + s
        for j in range(2):
            near_copy(plane, j).wait_recv()
        for r in range(GROUP):
            kept = part[plane, q, r]
            sent = near_in[s, r % 2]
            where = pl.ds((s * GROUP + r) * rows, rows)
            out[:, where] = jnp.where(x == r // 2, kept, sent) / samples

        @pl.when(plane != z)
        def _():
            for r in range(GROUP):
                remote(
                    part.at[plane, q, r], far_in.at[s, r], far_send.at[plane, r], far_recv.at[s, r],
                    samp, 1 - x,
                ).wait_recv()
                where = pl.ds((s * GROUP + r) * rows, rows)
                out[:, where] = out[:, where] + far_in[s, r].T / samples

    for k in (1, 2, 3):
        for h in (0, 1):
            swap(k, h).wait_send()
    for d in range(1, planes):
        sum_copy(z, d).wait_send()

    def drain(t, carry):
        plane, r = t // GROUP, t % GROUP

        @pl.when((z > 0) & (plane >= z))
        def _():
            left(plane, r, other.at[plane, r]).wait_send()

        @pl.when((z < planes - 1) & (plane <= z))
        def _():
            right(plane, r, other.at[plane, r]).wait_send()

        for j in range(2):
            core_copy(plane, r, j).wait_send()
        y_copy(plane, r).wait_send()

        @pl.when(r // 2 != x)
        def _():
            x_copy(plane, r).wait_send()

        @pl.when((r // 2 == x) & (plane // per != x))
        def _():
            near_copy(plane, r).wait_send()

        @pl.when((r // 2 == x) & (plane != z))
        def _():
            far_copy(plane, r).wait_send()

        return carry

    lax.fori_loop(0, steps, drain, 0)


def lines(jacobian):
    rows, total = jacobian.shape
    count = lax.axis_size("samp")
    planes = count // GROUP
    per = planes // 2
    width = total // GROUP
    half = width // 2
    f32 = jnp.float32
    dma = pltpu.SemaphoreType.DMA
    body = functools.partial(kernel, planes, rows, width, float(rows * count))
    return pl.pallas_call(
        body,
        out_shape=jax.ShapeDtypeStruct((rows, per * GROUP * rows), f32),
        in_specs=[pl.BlockSpec(memory_space=pl.ANY)],
        out_specs=pl.BlockSpec(memory_space=pltpu.VMEM),
        scratch_shapes=[
            pltpu.VMEM((2, GROUP, rows, half), f32),
            pltpu.VMEM((2, GROUP, rows, half), jnp.bfloat16),
            pltpu.VMEM((2, GROUP, rows, half), jnp.bfloat16),
            pltpu.VMEM((planes, GROUP, rows, half), f32),
            pltpu.VMEM((planes, 2, 8, half), f32),
            pltpu.VMEM((2, 1, half), f32),
            pltpu.VMEM((planes, GROUP, GROUP, rows, rows), f32),
            pltpu.VMEM((planes, GROUP, 2, rows, rows), f32),
            pltpu.VMEM((planes, GROUP, rows, rows), f32),
            pltpu.VMEM((planes, 2, rows, rows), f32),
            pltpu.VMEM((per, 2, rows, rows), f32),
            pltpu.VMEM((per, GROUP, rows, rows), f32),
            dma((2,)),
            dma((GROUP, 2)), dma((GROUP, 2)),
            dma((planes,)), dma((planes,)),
            dma((2, planes, GROUP)), dma((planes, GROUP)),
            dma((planes, GROUP, 2)), dma((planes, GROUP, 2)),
            dma((planes, GROUP)), dma((planes, GROUP)),
            dma((planes, GROUP)), dma((planes, GROUP)),
            dma((planes, GROUP)), dma((per, 2)),
            dma((planes, GROUP)), dma((per, GROUP)),
        ],
        compiler_params=pltpu.CompilerParams(
            collective_id=0, has_side_effects=True, vmem_limit_bytes=60 * 2**20
        ),
    )(jacobian)


def tile_product(a, b):
    return jnp.dot(a, b.T, preferred_element_type=jnp.float32, precision=lax.Precision.HIGHEST)


def gathered(jacobian):
    rows = jacobian.shape[0]
    samples = rows * lax.axis_size("samp")
    totals = lax.psum(jnp.sum(jacobian, axis=0), "samp")
    centred = jacobian - (totals / samples)[None, :]
    partial_rows = tile_product(centred, lax.all_gather(centred, "samp", axis=0, tiled=True))
    return lax.psum_scatter(partial_rows, "par", scatter_dimension=1, tiled=True) / samples


def scratch_bytes(rows, total, planes):
    square = rows * rows * 4
    return rows * total * 4 * 2 + planes * rows * total * 2 + planes * square * 30 + planes * square * 5


def solution(mesh):
    planes, rest = divmod(mesh.shape["samp"], GROUP)

    def per_device(jacobian):
        rows, total = jacobian.shape
        fits = scratch_bytes(rows, total, planes) <= 56 * 2**20
        if mesh.shape["par"] == 2 and rest == 0 and planes % 2 == 0 and fits and total % 1024 == 0:
            return lines(jacobian)
        return gathered(jacobian)

    return jax.shard_map(
        per_device, mesh=mesh, in_specs=(P("samp", "par"),), out_specs=P("samp", "par"), check_vma=False
    )
```
